256 devices in a mesh: leaf: 64 (over y, z, core), bond: 4 (over x).
Axes of the slice: x: 4, y: 4, z: 8, core: 2. Of those that a mesh axis runs over, the one named last changes fastest.
Arguments:
- leaf_metric: float32 [4, 256, 1024], P('bond', 'leaf'), may hold values from -257 to 257, as said below
- local_iso: float32 [192, 32, 1024], P('leaf', 'bond'), may hold values from -6 to 6
- top_iso: float32 [64, 32, 1024], P('leaf', 'bond'), may hold values from -6 to 6
Outputs:
- leaf_rho: float32 [4, 256, 1024], P('bond', 'leaf')
- inner_rho: float32 [4, 192, 1024], P('bond', 'leaf')
- top_rho: float32 [4, 64, 1024], P('bond', 'leaf')
The draws below stay inside these ranges and needn't reach their ends.
Inputs may be any that keep to these rules, and one draw needn't show every extreme that they name: Each entry of leaf_metric, taken as a 32 x 32 matrix, is symmetric positive definite.
All inputs are finite; a program needn't handle non-finite values.
Results may differ from the reference program's by a relative error of at most 0.0003.
Values sent between devices are 32-bit elements; how exact they have to be, the bound alone decides.
No kernel may reach another device: no remote copies, remote signals or barrier semaphores. Data moves between devices by JAX's collectives and lax.ppermute only.
A program may use at most 64 MiB of HBM per device.

```python
import math
import jax
import jax.numpy as jnp
from jax import lax

CHI = 32
LEAVES_DEV = 4
CHI2 = 1024
LEAVES = 256
INNER = 192
BATCH = 4
N_LEAF = 64


def draw_leaf_metric(key, part):
    first_key, second_key = jax.random.split(key)
    base = jax.random.truncated_normal(first_key, -4.0, 4.0, (BATCH, LEAVES, CHI, CHI), jnp.float32)
    spread = jax.random.uniform(second_key, (BATCH, LEAVES, CHI), jnp.float32, math.log(0.4), math.log(2.5))
    rows = base * jnp.exp(spread)[..., None]
    metric = jnp.einsum('mlac,mlbc->mlab', rows, rows) / CHI + 0.5 * jnp.eye(CHI, dtype=jnp.float32)
    return metric.reshape(BATCH, LEAVES, CHI2)


def isometry_law(key, node_rows):
    keys = jax.random.split(key, 4)
    left_gain = jax.random.truncated_normal(keys[0], -4.0, 4.0, (node_rows, CHI), jnp.float32) / math.sqrt(CHI)
    right_gain = jax.random.truncated_normal(keys[1], -4.0, 4.0, (node_rows, CHI), jnp.float32) / math.sqrt(CHI)
    identity = jnp.eye(CHI, dtype=jnp.float32)
    structured = identity[None, :, :, None] * left_gain[:, None, None, :] + identity[None, :, None, :] * right_gain[:, None, :, None]
    noise = jax.random.truncated_normal(keys[2], -4.0, 4.0, (node_rows, CHI, CHI, CHI), jnp.float32) / CHI
    parent_scale = jnp.exp(jax.random.uniform(keys[3], (node_rows, CHI), jnp.float32, math.log(0.5), math.log(2.0)))
    return ((structured + noise) * parent_scale[:, :, None, None]).reshape(node_rows, CHI, CHI2)


def draw_local_iso(key, part):
    return isometry_law(jax.random.fold_in(key, 11), INNER)


def draw_top_iso(key, part):
    base_key = jax.random.fold_in(key, 23)
    levels = N_LEAF.bit_length() - 1
    blocks = []
    for height in range(1, levels + 1):
        groups = N_LEAF >> height
        logical = isometry_law(jax.random.fold_in(base_key, height), groups)
        width = CHI2 >> height
        shares = jnp.transpose(logical.reshape(groups, CHI, 2 ** height, width), (0, 2, 1, 3))
        blocks.append(shares.reshape(N_LEAF, CHI, width))
    root_tensor = isometry_law(jax.random.fold_in(base_key, 99), 1)
    width = CHI2 >> levels
    blocks.append(jnp.transpose(root_tensor.reshape(CHI, N_LEAF, width), (1, 0, 2)))
    return jnp.concatenate(blocks, axis=2)


def setup_inputs(seed: int = 0) -> dict:
    streams_of = jax.random.split(jax.random.key(seed), 4)
    return {
        "leaf_metric": draw_leaf_metric(jax.random.fold_in(streams_of[3], 71), 0),
        "local_iso": draw_local_iso(jax.random.fold_in(streams_of[3], 71), 0),
        "top_iso": draw_top_iso(jax.random.fold_in(streams_of[3], 71), 0),
    }


exact_mode = lax.Precision.HIGHEST


def normalize(matrix):
    trace_value = jnp.trace(matrix, axis1=-2, axis2=-1)
    return matrix * (CHI / trace_value)[..., None, None]


def grow(tensor, left_env, right_env):
    first = jnp.einsum('npab,mnac->mnpcb', tensor, left_env, precision=exact_mode)
    second = jnp.einsum('mnpcb,mnbd->mnpcd', first, right_env, precision=exact_mode)
    third = jnp.einsum('mnpcd,nqcd->mnpq', second, tensor, precision=exact_mode)
    return normalize(third)


def descend(tensor, parent_state, left_env, right_env):
    mixed = jnp.einsum('mnpq,npab->mnqab', parent_state, tensor, precision=exact_mode)
    left_part = jnp.einsum('mnqab,mnbd->mnqad', mixed, right_env, precision=exact_mode)
    left_state = jnp.einsum('mnqad,nqcd->mnac', left_part, tensor, precision=exact_mode)
    right_part = jnp.einsum('mnqab,mnac->mnqcb', mixed, left_env, precision=exact_mode)
    right_state = jnp.einsum('mnqcb,nqcd->mnbd', right_part, tensor, precision=exact_mode)
    return normalize(left_state), normalize(right_state)


def blockwise(function, tensor, *matrices):
    node_total = tensor.shape[0]
    per_block = min(node_total, 16)
    groups = node_total // per_block
    grouped_tensor = tensor.reshape((groups, per_block) + tensor.shape[1:])
    grouped = [jnp.moveaxis(item.reshape((item.shape[0], groups, per_block) + item.shape[2:]), 1, 0) for item in matrices]

    def apply_block(operands):
        return function(operands[0], *operands[1:])

    result = lax.map(apply_block, tuple([grouped_tensor] + grouped))

    def restore(item):
        moved = jnp.moveaxis(item, 0, 1)
        return moved.reshape((moved.shape[0], node_total) + moved.shape[3:])

    return jax.tree.map(restore, result)


def unpack_level(top_iso, height):
    width = CHI2 >> height
    start = CHI2 - (CHI2 >> (height - 1))
    block = top_iso[:, :, start:start + width]
    groups = N_LEAF >> height
    block = block.reshape(groups, 2 ** height, CHI, width)
    return jnp.transpose(block, (0, 2, 1, 3)).reshape(groups, CHI, CHI, CHI)


def unpack_root(top_iso, levels):
    width = CHI2 >> levels
    block = top_iso[:, :, CHI2 - width:]
    return jnp.transpose(block, (1, 0, 2)).reshape(CHI, CHI, CHI)


def reference(leaf_metric, local_iso, top_iso):
    levels_dev = LEAVES_DEV.bit_length() - 1
    top_levels = N_LEAF.bit_length() - 1
    leaves = leaf_metric.reshape(BATCH, LEAVES, CHI, CHI)
    local_all = local_iso.reshape(N_LEAF, LEAVES_DEV - 1, CHI, CHI, CHI)
    tensors = []
    for height in range(1, levels_dev + 1):
        node_count = LEAVES_DEV >> height
        offset = LEAVES_DEV - 2 * node_count
        tensors.append(local_all[:, offset:offset + node_count].reshape(-1, CHI, CHI, CHI))
    for height in range(1, top_levels + 1):
        tensors.append(unpack_level(top_iso, height))
    envs = [leaves]
    for tensor in tensors:
        current = envs[-1]
        envs.append(blockwise(grow, tensor, current[:, 0::2], current[:, 1::2]))
    root_env = envs[-1][:, 0]
    root_tensor = unpack_root(top_iso, top_levels)
    gram = jnp.einsum('pab,qab->pq', root_tensor, root_tensor, precision=exact_mode)
    state = jnp.broadcast_to(normalize(gram), (BATCH, 1, CHI, CHI))
    total = len(tensors)
    collected = [state] * (total + 1)
    for level_index in range(total - 1, -1, -1):
        children = envs[level_index]
        left_state, right_state = blockwise(descend, tensors[level_index], state, children[:, 0::2], children[:, 1::2])
        state = jnp.stack([left_state, right_state], axis=2).reshape(BATCH, -1, CHI, CHI)
        collected[level_index] = state
    top = jnp.zeros((BATCH, N_LEAF, CHI, CHI), jnp.float32)
    for height in range(1, top_levels + 1):
        top = top.at[:, 2 ** (height - 1) - 1::2 ** height].set(collected[levels_dev + height])
    top = top.at[:, N_LEAF - 1].set(root_env)
    inner = jnp.zeros((BATCH, N_LEAF, LEAVES_DEV - 1, CHI, CHI), jnp.float32)
    for height in range(1, levels_dev + 1):
        node_count = LEAVES_DEV >> height
        offset = LEAVES_DEV - 2 * node_count
        inner = inner.at[:, :, offset:offset + node_count].set(collected[height].reshape(BATCH, N_LEAF, node_count, CHI, CHI))
    leaf_rho = collected[0].reshape(BATCH, LEAVES, CHI2)
    inner_rho = inner.reshape(BATCH, INNER, CHI2)
    top_rho = top.reshape(BATCH, N_LEAF, CHI2)
    return (leaf_rho, inner_rho, top_rho)
```

```python
import functools

import jax
import jax.numpy as jnp
from jax import lax
from jax.experimental import pallas as pl
from jax.experimental.pallas import tpu as pltpu
from jax.sharding import PartitionSpec as P

CHI = 32
LEAVES_DEV = 4
CHI2 = 1024
LANES = 128
CHUNKS = CHI2 // LANES
BF = jnp.bfloat16
F32 = jnp.float32


def lane_group(shape):
    return lax.broadcasted_iota(jnp.int32, shape, len(shape) - 1) // CHI


def halves(x):
    high = x.astype(BF).astype(F32)
    return high, x - high


def swap(chunks, first, second):
    for c in range(CHUNKS):
        first[c * CHI : (c + 1) * CHI, :] = chunks[c]
    group = lane_group((8, LANES))
    for c in range(CHUNKS):
        rows = [first[pl.ds(c * CHI + h, 8, stride=4), :] for h in range(4)]
        for g in range(4):
            moved = [pltpu.roll(rows[h], CHI * ((h - g) % 4), 1) if h != g else rows[h] for h in range(4)]
            low = jnp.where(group == 0, moved[0], moved[1])
            high = jnp.where(group == 2, moved[2], moved[3])
            second[(4 * c + g) * 8 : (4 * c + g) * 8 + 8, :] = jnp.where(group < 2, low, high)
    return [second[pl.ds(c, CHI, stride=8), :] for c in range(CHUNKS)]


def transposed(chunks):
    result = []
    for i in range(2):
        block = jnp.concatenate(chunks[4 * i : 4 * i + 4], axis=0).T
        result += [block[CHI * g : CHI * (g + 1)] for g in range(4)]
    return result


def swap_back(chunks, first, second):
    for c in range(CHUNKS):
        first[c * CHI : (c + 1) * CHI, :] = chunks[c]
    group = lane_group((8, LANES))
    for c in range(CHUNKS):
        rows = [first[pl.ds(c * CHI + h, 8, stride=4), :] for h in range(4)]
        for j in range(4):
            moved = [pltpu.roll(rows[h], CHI * ((h - j) % 4), 1) if h != j else rows[h] for h in range(4)]
            low = jnp.where(group == 0, moved[0], moved[1])
            high = jnp.where(group == 2, moved[2], moved[3])
            a = 16 * (c // 4) + 4 * j + c % 4
            second[a * 8 : a * 8 + 8, :] = jnp.where(group < 2, low, high)
    return [second[pl.ds(c, CHI, stride=8), :] for c in range(CHUNKS)]


def split_rows(chunks):
    pairs = [halves(c) for c in chunks]
    high = jnp.concatenate([p[0] for p in pairs], axis=1)
    low = jnp.concatenate([p[1] for p in pairs], axis=1)
    return jnp.concatenate([high, low], axis=0).astype(BF)


def split_lanes(chunks):
    high, low = halves(jnp.concatenate(chunks, axis=0))
    return jnp.concatenate([high, low], axis=1).astype(BF)


def left_multiply(matrix, split):
    high, low = halves(matrix)
    left = jnp.where(lane_group(matrix.shape) < 2, high, low).astype(BF)
    right = jnp.concatenate([split, split], axis=0)
    out = jnp.dot(left, right, preferred_element_type=F32)
    return [out[:, LANES * c : LANES * (c + 1)] for c in range(CHUNKS)]


def right_multiply(split, matrix):
    shape = (LANES, LANES)
    keep = lax.broadcasted_iota(jnp.int32, shape, 0) // CHI == lane_group(shape)
    blocks = [
        jnp.where(keep, jnp.concatenate([part] * 4, axis=0), 0.0).astype(BF) for part in halves(matrix)
    ]
    row = jnp.concatenate(blocks, axis=1)
    out = jnp.dot(split, jnp.concatenate([row, row], axis=0), preferred_element_type=F32)
    out = out[:, :LANES] + out[:, LANES:]
    return [out[CHI * c : CHI * (c + 1)] for c in range(CHUNKS)]


def contract(left, right):
    high, low = right[:CHI], right[CHI:]
    wide = jnp.concatenate([high] * 4 + [low] * 4, axis=0)
    out = lax.dot_general(left, wide, (((1,), (1,)), ((), ())), preferred_element_type=F32)
    out = out[:CHI] + out[CHI:]
    return out[:, :LANES] + out[:, LANES:]


def normalize(matrix):
    row = lax.broadcasted_iota(jnp.int32, matrix.shape, 0)
    lane = lax.broadcasted_iota(jnp.int32, matrix.shape, 1)
    diagonal = jnp.where(row == lane, matrix, 0.0)
    trace = jnp.sum(jnp.sum(diagonal, axis=1, keepdims=True), axis=0, keepdims=True)
    return matrix * (CHI / trace)


def grow(natural_split, moved_split, left_env, right_env, first, second):
    turned = swap(left_multiply(left_env, moved_split), first, second)
    both = right_multiply(split_lanes(turned), right_env)
    return normalize(contract(split_rows(both), natural_split))


def load_chunks(ref):
    return [ref[:, LANES * c : LANES * (c + 1)] for c in range(CHUNKS)]


def scratch_pair():
    return [pltpu.VMEM((CHUNKS * CHI, LANES), F32), pltpu.VMEM((CHUNKS * CHI, LANES), F32)]


def full_spec():
    return pl.BlockSpec(memory_space=pltpu.VMEM)


def scalar_spec():
    return pl.BlockSpec(memory_space=pltpu.SMEM)


def shape_of(*shape, dtype=F32):
    return jax.ShapeDtypeStruct(shape, dtype)


ENV = (CHI, LANES)
ROWS = (2 * CHI, CHI2)
WIDE = (CHUNKS * CHI, 2 * LANES)


def kernel_call(kernel, outs, in_specs, args, scratch, nanos):
    return pl.pallas_call(
        kernel,
        out_shape=outs,
        in_specs=in_specs,
        out_specs=[full_spec()] * len(outs),
        scratch_shapes=scratch,
        cost_estimate=pl.CostEstimate(flops=int(nanos * 1000), bytes_accessed=1024 * 256, transcendentals=0),
        compiler_params=pltpu.CompilerParams(vmem_limit_bytes=24 * 1024 * 1024),
    )(*args)


def prepare_kernel(upper_ref, iso_ref, natural_ref, moved_ref, own_ref, other_ref, first, second):
    natural = load_chunks(iso_ref)
    natural_ref[...] = split_rows(natural)
    moved_ref[...] = split_rows(swap(natural, first, second))
    by_left = swap_back(transposed(natural), first, second)
    by_right = swap(by_left, first, second)
    upper = upper_ref[0] == 1
    own = [jnp.where(upper, r, l) for l, r in zip(by_left, by_right)]
    other = [jnp.where(upper, l, r) for l, r in zip(by_left, by_right)]
    own_ref[...] = split_lanes(own)
    other_ref[...] = split_rows(other)


def prepare(upper, iso):
    outs = [shape_of(*ROWS, dtype=BF), shape_of(*ROWS, dtype=BF), shape_of(*WIDE, dtype=BF), shape_of(*ROWS, dtype=BF)]
    return kernel_call(prepare_kernel, outs, [scalar_spec(), full_spec()], (upper, iso), scratch_pair(), 1000)


def grow_kernel(upper_ref, natural_ref, moved_ref, env_ref, sibling_ref, out_ref, first, second):
    upper = upper_ref[0] == 1
    env, sibling = env_ref[...], sibling_ref[...]
    left_env = jnp.where(upper, sibling, env)
    right_env = jnp.where(upper, env, sibling)
    out_ref[...] = grow(natural_ref[...], moved_ref[...], left_env, right_env, first, second)


def grow_level(upper, natural, moved, env, sibling):
    specs = [scalar_spec()] + [full_spec()] * 4
    return kernel_call(
        grow_kernel, [shape_of(*ENV)], specs, (upper, natural, moved, env, sibling), scratch_pair(), 1000
    )[0]


def partner_kernel(other_ref, sibling_ref, out_ref, first, second):
    out_ref[...] = split_rows(swap(left_multiply(sibling_ref[...], other_ref[...]), first, second))


def partner_level(other, sibling):
    outs = [shape_of(*ROWS, dtype=BF)]
    return kernel_call(partner_kernel, outs, [full_spec()] * 2, (other, sibling), scratch_pair(), 500)[0]


def local_kernel(leaf_ref, iso_ref, env_ref, top_env_ref, first, second):
    envs = []
    for node in range(3):
        natural = load_chunks(iso_ref.at[node])
        natural_split = split_rows(natural)
        moved_split = split_rows(swap(natural, first, second))
        if node < 2:
            pair = leaf_ref[2 * node], leaf_ref[2 * node + 1]
        else:
            pair = envs
        env = grow(natural_split, moved_split, *pair, first, second)
        envs.append(env)
    env_ref[0] = envs[0]
    env_ref[1] = envs[1]
    top_env_ref[...] = envs[2]


def local_edges_kernel(leaf_ref, env_ref, iso_ref, own_ref, partner_ref, first, second):
    for node in range(3):
        by_left = swap_back(transposed(load_chunks(iso_ref.at[node])), first, second)
        by_right = swap(by_left, first, second)
        if node < 2:
            left_env, right_env = leaf_ref[2 * node], leaf_ref[2 * node + 1]
        else:
            left_env, right_env = env_ref[0], env_ref[1]
        own_ref[2 * node] = split_lanes(by_left)
        own_ref[2 * node + 1] = split_lanes(by_right)
        left_split, right_split = split_rows(by_left), split_rows(by_right)
        partner_ref[2 * node] = split_rows(swap(left_multiply(right_env, right_split), first, second))
        partner_ref[2 * node + 1] = split_rows(swap(left_multiply(left_env, left_split), first, second))


def flat(matrix, first):
    first[0:CHI, :] = matrix
    group = lane_group((8, LANES))
    rows = [first[pl.ds(h, 8, stride=4), :] for h in range(4)]
    return jnp.where(group < 2, jnp.where(group == 0, rows[0], rows[1]), jnp.where(group == 2, rows[2], rows[3]))


def write_flat(out_ref, index, flattened):
    for c in range(CHUNKS):
        out_ref[index : index + 1, LANES * c : LANES * (c + 1)] = flattened[c : c + 1, :]


def descend(own, partner, state):
    mixed = right_multiply(own, state)
    return normalize(contract(split_rows(mixed), partner))


def down_kernel(levels, marked_ref, root_ref, env_ref, *refs):
    own_refs, partner_refs = refs[:levels], refs[levels : 2 * levels]
    local_own, local_partner, leaf_out, inner_out, top_out, first = refs[2 * levels :]
    gram = split_rows(load_chunks(root_ref))
    state = normalize(contract(gram, gram))
    top = env_ref[...]
    for level in range(levels - 1, -1, -1):
        top = jnp.where(marked_ref[level] == 1, state, top)
        state = descend(own_refs[level][...], partner_refs[level][...], state)
    write_flat(top_out, 0, flat(top, first))
    states = [None, None, state]
    for node in (2, 1, 0):
        write_flat(inner_out, node, flat(states[node], first))
        for side in range(2):
            child = descend(local_own[2 * node + side], local_partner[2 * node + side], states[node])
            if node == 2:
                states[side] = child
            else:
                write_flat(leaf_out, 2 * node + side, flat(child, first))


def exchange(value, mask):
    pairs = [(source, source ^ mask) for source in range(lax.axis_size("leaf"))]
    return lax.ppermute(value, "leaf", pairs)


def gather_bond(value):
    size = lax.axis_size("bond")
    mine = lax.axis_index("bond")
    whole = jnp.zeros((size, *value.shape), value.dtype)
    whole = lax.dynamic_update_index_in_dim(whole, value, mine, 0)
    for mask in range(1, size):
        pairs = [(source, source ^ mask) for source in range(size)]
        whole = lax.dynamic_update_index_in_dim(whole, lax.ppermute(value, "bond", pairs), mine ^ mask, 0)
    return whole


def body(leaf_metric, local_iso, top_iso):
    devices = lax.axis_size("leaf")
    top_levels = devices.bit_length() - 1
    position = lax.axis_index("leaf")
    uppers = [(position >> level & 1).astype(jnp.int32).reshape(1) for level in range(top_levels)]
    leaves = jnp.tile(leaf_metric.reshape(LEAVES_DEV, CHI, CHI), (1, 1, 4))

    gathered = gather_bond(jnp.concatenate([local_iso, top_iso], axis=0))
    gathered = jnp.moveaxis(gathered, 0, 1).reshape(LEAVES_DEV, CHI, CHI2)
    local_whole, packed = gathered[: LEAVES_DEV - 1], gathered[LEAVES_DEV - 1]

    local_envs, env = kernel_call(
        local_kernel,
        [shape_of(2, *ENV), shape_of(*ENV)],
        [full_spec()] * 2,
        (leaves, local_whole),
        scratch_pair(),
        3000,
    )
    local_own, local_partner = kernel_call(
        local_edges_kernel,
        [shape_of(6, *WIDE, dtype=BF), shape_of(6, *ROWS, dtype=BF)],
        [full_spec()] * 3,
        (leaves, local_envs, local_whole),
        scratch_pair(),
        4000,
    )

    shares = []
    for height in range(1, top_levels + 1):
        start = CHI2 - (CHI2 >> height - 1)
        shares.append(packed[:, start : start + (CHI2 >> height)])
    shares.append(packed[:, CHI2 - (CHI2 >> top_levels) :])
    for level in range(top_levels):
        pending = shares[level:]
        incoming = exchange(jnp.concatenate(pending, axis=1), 1 << level)
        upper = uppers[level][0] == 1
        merged = []
        cursor = 0
        for mine in pending:
            breadth = mine.shape[1]
            theirs = incoming[:, cursor : cursor + breadth]
            cursor += breadth
            merged.append(
                jnp.where(
                    upper,
                    jnp.concatenate([theirs, mine], axis=1),
                    jnp.concatenate([mine, theirs], axis=1),
                )
            )
        shares = shares[:level] + merged

    masks = [1, 2, 4, 12, 16, 48]
    owns, partners = [], []
    for level in range(top_levels):
        natural, moved, own, other = prepare(uppers[level], shares[level])
        sibling = exchange(env, masks[level] if level < len(masks) else 1 << level)
        env = grow_level(uppers[level], natural, moved, env, sibling)
        owns.append(own)
        partners.append(partner_level(other, sibling))

    marked = jnp.stack(
        [((position + 1) % (2 << level) == 1 << level).astype(jnp.int32) for level in range(top_levels)]
    )
    leaf_rho, inner_rho, top_rho = kernel_call(
        functools.partial(down_kernel, top_levels),
        [shape_of(LEAVES_DEV, CHI2), shape_of(LEAVES_DEV - 1, CHI2), shape_of(1, CHI2)],
        [scalar_spec()] + [full_spec()] * (2 * top_levels + 4),
        (marked, shares[top_levels], env, *owns, *partners, local_own, local_partner),
        [pltpu.VMEM((CHI, LANES), F32)],
        8000,
    )
    return (leaf_rho[None], inner_rho[None], top_rho[None])


def solution(mesh):
    in_specs = (P("bond", "leaf", None), P("leaf", "bond", None), P("leaf", "bond", None))
    out_specs = (P("bond", "leaf", None), P("bond", "leaf", None), P("bond", "leaf", None))
    return jax.shard_map(body, mesh=mesh, in_specs=in_specs, out_specs=out_specs, check_vma=False)
```

```python
import functools

import jax
import jax.numpy as jnp
from jax import lax
from jax.experimental import pallas as pl
from jax.experimental.pallas import tpu as pltpu
from jax.sharding import PartitionSpec as P

CHI = 32
LEAVES_DEV = 4
CHI2 = 1024
LANES = 128
CHUNKS = CHI2 // LANES
BF = jnp.bfloat16
F32 = jnp.float32


def lane_group(shape):
    return lax.broadcasted_iota(jnp.int32, shape, len(shape) - 1) // CHI


def halves(x):
    high = x.astype(BF).astype(F32)
    return high, x - high


def swap(chunks, first, second):
    for c in range(CHUNKS):
        first[c * CHI : (c + 1) * CHI, :] = chunks[c]
    group = lane_group((8, LANES))
    for c in range(CHUNKS):
        rows = [first[pl.ds(c * CHI + h, 8, stride=4), :] for h in range(4)]
        for g in range(4):
            moved = [pltpu.roll(rows[h], CHI * ((h - g) % 4), 1) if h != g else rows[h] for h in range(4)]
            low = jnp.where(group == 0, moved[0], moved[1])
            high = jnp.where(group == 2, moved[2], moved[3])
            second[(4 * c + g) * 8 : (4 * c + g) * 8 + 8, :] = jnp.where(group < 2, low, high)
    return [second[pl.ds(c, CHI, stride=8), :] for c in range(CHUNKS)]


def transposed(chunks):
    result = []
    for i in range(2):
        block = jnp.concatenate(chunks[4 * i : 4 * i + 4], axis=0).T
        result += [block[CHI * g : CHI * (g + 1)] for g in range(4)]
    return result


def swap_back(chunks, first, second):
    for c in range(CHUNKS):
        first[c * CHI : (c + 1) * CHI, :] = chunks[c]
    group = lane_group((8, LANES))
    for c in range(CHUNKS):
        rows = [first[pl.ds(c * CHI + h, 8, stride=4), :] for h in range(4)]
        for j in range(4):
            moved = [pltpu.roll(rows[h], CHI * ((h - j) % 4), 1) if h != j else rows[h] for h in range(4)]
            low = jnp.where(group == 0, moved[0], moved[1])
            high = jnp.where(group == 2, moved[2], moved[3])
            a = 16 * (c // 4) + 4 * j + c % 4
            second[a * 8 : a * 8 + 8, :] = jnp.where(group < 2, low, high)
    return [second[pl.ds(c, CHI, stride=8), :] for c in range(CHUNKS)]


def split_rows(chunks):
    pairs = [halves(c) for c in chunks]
    high = jnp.concatenate([p[0] for p in pairs], axis=1)
    low = jnp.concatenate([p[1] for p in pairs], axis=1)
    return jnp.concatenate([high, low], axis=0).astype(BF)


def split_lanes(chunks):
    high, low = halves(jnp.concatenate(chunks, axis=0))
    return jnp.concatenate([high, low], axis=1).astype(BF)


def left_multiply(matrix, split):
    high, low = halves(matrix)
    left = jnp.where(lane_group(matrix.shape) < 2, high, low).astype(BF)
    right = jnp.concatenate([split, split], axis=0)
    out = jnp.dot(left, right, preferred_element_type=F32)
    return [out[:, LANES * c : LANES * (c + 1)] for c in range(CHUNKS)]


def right_multiply(split, matrix):
    shape = (LANES, LANES)
    keep = lax.broadcasted_iota(jnp.int32, shape, 0) // CHI == lane_group(shape)
    blocks = [
        jnp.where(keep, jnp.concatenate([part] * 4, axis=0), 0.0).astype(BF) for part in halves(matrix)
    ]
    row = jnp.concatenate(blocks, axis=1)
    out = jnp.dot(split, jnp.concatenate([row, row], axis=0), preferred_element_type=F32)
    out = out[:, :LANES] + out[:, LANES:]
    return [out[CHI * c : CHI * (c + 1)] for c in range(CHUNKS)]


def contract(left, right):
    high, low = right[:CHI], right[CHI:]
    wide = jnp.concatenate([high, high, low, low], axis=0)
    out = lax.dot_general(left, wide, (((1,), (1,)), ((), ())), preferred_element_type=F32)
    out = out[:CHI] + out[CHI:]
    return out + pltpu.roll(out, LANES // 2, 1)


def normalize(matrix):
    row = lax.broadcasted_iota(jnp.int32, matrix.shape, 0)
    lane = lax.broadcasted_iota(jnp.int32, matrix.shape, 1)
    diagonal = jnp.where(row == lane, matrix, 0.0)
    trace = jnp.sum(jnp.sum(diagonal, axis=0, keepdims=True), axis=1, keepdims=True)
    return matrix * (CHI / trace)


def grow(natural_split, moved_split, left_env, right_env, first, second):
    turned = swap(left_multiply(left_env, moved_split), first, second)
    both = right_multiply(split_lanes(turned), right_env)
    return normalize(contract(split_rows(both), natural_split))


def load_chunks(ref):
    return [ref[:, LANES * c : LANES * (c + 1)] for c in range(CHUNKS)]


def scratch_pair():
    return [pltpu.VMEM((CHUNKS * CHI, LANES), F32), pltpu.VMEM((CHUNKS * CHI, LANES), F32)]


def full_spec():
    return pl.BlockSpec(memory_space=pltpu.VMEM)


def scalar_spec():
    return pl.BlockSpec(memory_space=pltpu.SMEM)


def shape_of(*shape, dtype=F32):
    return jax.ShapeDtypeStruct(shape, dtype)


ENV = (CHI, LANES)
MESSAGE = (CHI + 8, LANES)
ROWS = (2 * CHI, CHI2)
WIDE = (CHUNKS * CHI, 2 * LANES)
HALF = (CHI, CHI2 // 2)


def kernel_call(kernel, outs, scalars, args, scratch, nanos):
    return pl.pallas_call(
        kernel,
        out_shape=outs,
        in_specs=[scalar_spec()] * len(scalars) + [full_spec()] * len(args),
        out_specs=[full_spec()] * len(outs),
        scratch_shapes=scratch,
        cost_estimate=pl.CostEstimate(flops=int(nanos * 1150000), bytes_accessed=1024, transcendentals=0),
        compiler_params=pltpu.CompilerParams(vmem_limit_bytes=24 * 1024 * 1024),
    )(*scalars, *args)


def bond_rows(bond_ref, mask):
    return pl.ds(pl.multiple_of(8 * (bond_ref[0] ^ mask), 8), 8)


def assemble_kernel(bond_ref, *refs):
    *pieces, now_ref, later_ref = refs
    for mask, piece in enumerate(pieces):
        rows = bond_rows(bond_ref, mask)
        now_ref[rows, :] = piece[LEAVES_DEV - 1, :, : CHI2 // 2]
        later_ref[rows, :] = piece[LEAVES_DEV - 1, :, CHI2 // 2 :]


def interleave(low, high, width):
    chunks = []
    lane = lax.broadcasted_iota(jnp.int32, (CHI, LANES), 1)
    for c in range(CHUNKS):
        if width >= LANES:
            block, rest = LANES * c // width, LANES * c % width
            part = high if block % 2 else low
            chunks.append(part[(block // 2 * width + rest) // LANES])
            continue
        base = LANES // 2 * (c % 2)
        out = None
        for block in range(LANES // width):
            part = (high if block % 2 else low)[c // 2]
            shift = (block * width - base - block // 2 * width) % LANES
            moved = pltpu.roll(part, shift, 1) if shift else part
            out = moved if out is None else jnp.where(lane < block * width, out, moved)
        chunks.append(out)
    return chunks


def every_other(chunks, width, parity):
    half = len(chunks) // 2
    if width >= LANES:
        step = width // LANES
        return [c for i, c in enumerate(chunks) if i // step % 2 == parity]
    lane = lax.broadcasted_iota(jnp.int32, (CHI, LANES), 1)
    groups = LANES // width
    result = []
    for i in range(half):
        out = None
        for j in range(groups):
            source = 2 * j + parity
            shift = (j - source) * width % LANES
            part = chunks[2 * i + source // groups]
            moved = pltpu.roll(part, shift, 1) if shift else part
            out = moved if out is None else jnp.where(lane < j * width, out, moved)
        result.append(out)
    return result


def merge_kernel(width, upper_ref, mine_ref, theirs_ref, after_ref, now_ref, *later_refs):
    upper = upper_ref[0] == 1
    mine = [mine_ref[:, LANES * c : LANES * (c + 1)] for c in range(CHUNKS // 2)]
    theirs = [theirs_ref[:, LANES * c : LANES * (c + 1)] for c in range(CHUNKS // 2)]
    low = [jnp.where(upper, t, m) for m, t in zip(mine, theirs)]
    high = [jnp.where(upper, m, t) for m, t in zip(mine, theirs)]
    for parity, out_ref in enumerate((now_ref, *later_refs)):
        out = every_other(low, width, parity) + every_other(high, width, parity)
        for c, chunk in enumerate(out):
            out_ref[:, LANES * c : LANES * (c + 1)] = chunk


def merge(width, upper, mine, theirs, after, last):
    outs = [shape_of(*HALF)] * (1 if last else 2)
    return kernel_call(
        functools.partial(merge_kernel, width), outs, (upper,), (mine, theirs, after), [], 300
    )


def prepare_kernel(
    width, core_ref, upper_ref, mine_ref, theirs_ref, natural_ref, moved_ref, own_ref, other_ref, first, second
):
    core = core_ref[0] == 1
    mine = [mine_ref[:, LANES * c : LANES * (c + 1)] for c in range(CHUNKS // 2)]
    theirs = [theirs_ref[:, LANES * c : LANES * (c + 1)] for c in range(CHUNKS // 2)]
    low = [jnp.where(core, t, m) for m, t in zip(mine, theirs)]
    high = [jnp.where(core, m, t) for m, t in zip(mine, theirs)]
    natural = interleave(low, high, width)
    natural_ref[...] = split_rows(natural)
    moved_ref[...] = split_rows(swap(natural, first, second))
    by_left = swap_back(transposed(natural), first, second)
    by_right = swap(by_left, first, second)
    upper = upper_ref[0] == 1
    own = [jnp.where(upper, r, l) for l, r in zip(by_left, by_right)]
    other = [jnp.where(upper, l, r) for l, r in zip(by_left, by_right)]
    own_ref[...] = split_lanes(own)
    other_ref[...] = split_rows(other)


def prepare(width, core, upper, mine, theirs):
    outs = [shape_of(*ROWS, dtype=BF), shape_of(*ROWS, dtype=BF), shape_of(*WIDE, dtype=BF), shape_of(*ROWS, dtype=BF)]
    return kernel_call(
        functools.partial(prepare_kernel, width), outs, (core, upper), (mine, theirs), scratch_pair(), 600
    )


def grow_kernel(upper_ref, natural_ref, moved_ref, mine_ref, theirs_ref, out_ref, first, second):
    upper = upper_ref[0] == 1
    mine, theirs = mine_ref[:CHI, :], theirs_ref[:CHI, :]
    left_env = jnp.where(upper, theirs, mine)
    right_env = jnp.where(upper, mine, theirs)
    out_ref[:CHI, :] = grow(natural_ref[...], moved_ref[...], left_env, right_env, first, second)
    out_ref[CHI:, :] = mine_ref[CHI:, :] + theirs_ref[CHI:, :]


def grow_level(upper, natural, moved, mine, theirs):
    return kernel_call(
        grow_kernel, [shape_of(*MESSAGE)], (upper,), (natural, moved, mine, theirs), scratch_pair(), 800
    )[0]


def partner_kernel(other_ref, theirs_ref, out_ref, first, second):
    out_ref[...] = split_rows(swap(left_multiply(theirs_ref[:CHI, :], other_ref[...]), first, second))


def partner_level(other, theirs):
    return kernel_call(partner_kernel, [shape_of(*ROWS, dtype=BF)], (), (other, theirs), scratch_pair(), 350)[0]


def local_kernel(root_width, bond_ref, leaf_ref, *refs):
    pieces = refs[:-5]
    iso_ref, env_ref, message_ref, first, second = refs[-5:]
    nodes = LEAVES_DEV - 1
    for mask, piece in enumerate(pieces):
        rows = bond_rows(bond_ref, mask)
        for node in range(nodes):
            iso_ref[node, rows, :] = piece[node]
        first[rows, :] = piece[nodes, :, CHI2 - LANES :]
    lane = lax.broadcasted_iota(jnp.int32, (CHI, LANES), 1)
    root = split_rows([jnp.where(lane >= LANES - root_width, first[:CHI, :], 0.0)])
    gram = contract(root, root)
    envs = []
    for node in range(nodes):
        natural = load_chunks(iso_ref.at[node])
        natural_split = split_rows(natural)
        moved_split = split_rows(swap(natural, first, second))
        if node < 2:
            pair = leaf_ref[2 * node], leaf_ref[2 * node + 1]
        else:
            pair = envs
        envs.append(grow(natural_split, moved_split, *pair, first, second))
    env_ref[0] = envs[0]
    env_ref[1] = envs[1]
    message_ref[:CHI, :] = envs[2]
    message_ref[CHI:, :] = flat(gram, first)


def local_edges_kernel(leaf_ref, env_ref, iso_ref, after_ref, own_ref, partner_ref, first, second):
    for node in range(LEAVES_DEV - 1):
        by_left = swap_back(transposed(load_chunks(iso_ref.at[node])), first, second)
        by_right = swap(by_left, first, second)
        if node < 2:
            left_env, right_env = leaf_ref[2 * node], leaf_ref[2 * node + 1]
        else:
            left_env, right_env = env_ref[0], env_ref[1]
        own_ref[2 * node] = split_lanes(by_left)
        own_ref[2 * node + 1] = split_lanes(by_right)
        left_split, right_split = split_rows(by_left), split_rows(by_right)
        partner_ref[2 * node] = split_rows(swap(left_multiply(right_env, right_split), first, second))
        partner_ref[2 * node + 1] = split_rows(swap(left_multiply(left_env, left_split), first, second))


def flat(matrix, first):
    first[0:CHI, :] = matrix
    group = lane_group((8, LANES))
    rows = [first[pl.ds(h, 8, stride=4), :] for h in range(4)]
    return jnp.where(group < 2, jnp.where(group == 0, rows[0], rows[1]), jnp.where(group == 2, rows[2], rows[3]))


def unflat(flattened, first):
    group = lane_group((8, LANES))
    for h in range(4):
        part = jnp.where(group == h, flattened, 0.0)
        part = part + pltpu.roll(part, CHI, 1)
        first[pl.ds(h, 8, stride=4), :] = part + pltpu.roll(part, 2 * CHI, 1)
    return first[0:CHI, :]


def write_flat(out_ref, index, flattened):
    for c in range(CHUNKS):
        out_ref[index, 0:1, LANES * c : LANES * (c + 1)] = flattened[c : c + 1, :]


def descend(own, partner, state):
    mixed = right_multiply(own, state)
    return normalize(contract(split_rows(mixed), partner))


def down_kernel(levels, marked_ref, message_ref, *refs):
    own_refs, partner_refs = refs[:levels], refs[levels : 2 * levels]
    local_own, local_partner, leaf_out, inner_out, top_out, first = refs[2 * levels :]
    state = normalize(unflat(message_ref[CHI:, :], first))
    top = message_ref[:CHI, :]
    for level in range(levels - 1, -1, -1):
        top = jnp.where(marked_ref[level] == 1, state, top)
        state = descend(own_refs[level][...], partner_refs[level][...], state)
    states = [None, None, state]
    children = []
    for node in (2, 1, 0):
        for side in range(2):
            child = descend(local_own[2 * node + side], local_partner[2 * node + side], states[node])
            if node == 2:
                states[side] = child
            else:
                children.append((2 * node + side, child))
    write_flat(top_out, 0, flat(top, first))
    for node in range(3):
        write_flat(inner_out, node, flat(states[node], first))
    for leaf, child in children:
        flattened = flat(child, first)
        for c in range(CHUNKS):
            leaf_out[leaf : leaf + 1, LANES * c : LANES * (c + 1)] = flattened[c : c + 1, :]


def exchange(value, mask):
    pairs = [(source, source ^ mask) for source in range(lax.axis_size("leaf"))]
    return lax.ppermute(value, "leaf", pairs)


def bond_pieces(value):
    size = lax.axis_size("bond")
    return [value] + [
        lax.ppermute(value, "bond", [(source, source ^ mask) for source in range(size)]) for mask in range(1, size)
    ]


def body(leaf_metric, local_iso, top_iso):
    devices = lax.axis_size("leaf")
    top_levels = devices.bit_length() - 1
    masks = [1, 2, 4, 12, 16, 48]
    position = lax.axis_index("leaf")
    bits = [(position >> level & 1).astype(jnp.int32).reshape(1) for level in range(top_levels)]
    bond = lax.axis_index("bond").astype(jnp.int32).reshape(1)
    leaves = jnp.tile(leaf_metric.reshape(LEAVES_DEV, CHI, CHI), (1, 1, 4))

    pieces = bond_pieces(jnp.concatenate([local_iso, top_iso], axis=0))
    now, later = kernel_call(assemble_kernel, [shape_of(*HALF)] * 2, (bond,), pieces, [], 200)
    local_whole, local_envs, message = kernel_call(
        functools.partial(local_kernel, CHI2 // devices),
        [shape_of(LEAVES_DEV - 1, CHI, CHI2), shape_of(2, *ENV), shape_of(*MESSAGE)],
        (bond,),
        (leaves, *pieces),
        scratch_pair(),
        2500,
    )

    owns, partners = [], []
    for level in range(top_levels):
        if level + 1 < top_levels:
            incoming = exchange(later, masks[level + 1])
        other_half = exchange(now, 1)
        natural, moved, own, other = prepare(CHI2 >> level + 1, bits[0], bits[level], now, other_half)
        theirs = exchange(message, masks[level])
        before = message
        message = grow_level(bits[level], natural, moved, message, theirs)
        if level + 1 < top_levels:
            last = level + 2 == top_levels
            now, *rest = merge(CHI2 >> level + 2, bits[level + 1], later, incoming, before, last)
            later = None if last else rest[0]
        if level == top_levels - 2:
            after = message
        owns.append(own)
        partners.append(partner_level(other, theirs))
    local_own, local_partner = kernel_call(
        local_edges_kernel,
        [shape_of(6, *WIDE, dtype=BF), shape_of(6, *ROWS, dtype=BF)],
        (),
        (leaves, local_envs, local_whole, after),
        scratch_pair(),
        2500,
    )

    marked = jnp.stack(
        [((position + 1) % (2 << level) == 1 << level).astype(jnp.int32) for level in range(top_levels)]
    )
    leaf_rho, inner_rho, top_rho = kernel_call(
        functools.partial(down_kernel, top_levels),
        [shape_of(LEAVES_DEV, CHI2), shape_of(LEAVES_DEV - 1, 1, CHI2), shape_of(1, 1, CHI2)],
        (marked,),
        (message, *owns, *partners, local_own, local_partner),
        [pltpu.VMEM((CHI, LANES), F32)],
        7000,
    )
    return (leaf_rho[None], jnp.swapaxes(inner_rho, 0, 1), top_rho)


def solution(mesh):
    in_specs = (P("bond", "leaf", None), P("leaf", "bond", None), P("leaf", "bond", None))
    out_specs = (P("bond", "leaf", None), P("bond", "leaf", None), P("bond", "leaf", None))
    return jax.shard_map(body, mesh=mesh, in_specs=in_specs, out_specs=out_specs, check_vma=False)
```

```python
import functools

import jax
import jax.numpy as jnp
from jax import lax
from jax.experimental import pallas as pl
from jax.experimental.pallas import tpu as pltpu
from jax.sharding import PartitionSpec as P

CHI = 32
LEAVES_DEV = 4
CHI2 = 1024
LANES = 128
CHUNKS = CHI2 // LANES
BOND_MASKS = (0, 2, 3, 1)
BF = jnp.bfloat16
F32 = jnp.float32


def lane_group(shape):
    return lax.broadcasted_iota(jnp.int32, shape, len(shape) - 1) // CHI


def halves(x):
    high = x.astype(BF).astype(F32)
    return high, x - high


def swap(chunks, first, second):
    for c in range(CHUNKS):
        first[c * CHI : (c + 1) * CHI, :] = chunks[c]
    group = lane_group((8, LANES))
    for c in range(CHUNKS):
        rows = [first[pl.ds(c * CHI + h, 8, stride=4), :] for h in range(4)]
        for g in range(4):
            moved = [pltpu.roll(rows[h], CHI * ((h - g) % 4), 1) if h != g else rows[h] for h in range(4)]
            low = jnp.where(group == 0, moved[0], moved[1])
            high = jnp.where(group == 2, moved[2], moved[3])
            second[(4 * c + g) * 8 : (4 * c + g) * 8 + 8, :] = jnp.where(group < 2, low, high)
    return [second[pl.ds(c, CHI, stride=8), :] for c in range(CHUNKS)]


def transposed(chunks):
    result = []
    for i in range(2):
        block = jnp.concatenate(chunks[4 * i : 4 * i + 4], axis=0).T
        result += [block[CHI * g : CHI * (g + 1)] for g in range(4)]
    return result


def swap_back(chunks, first, second):
    for c in range(CHUNKS):
        first[c * CHI : (c + 1) * CHI, :] = chunks[c]
    group = lane_group((8, LANES))
    for c in range(CHUNKS):
        rows = [first[pl.ds(c * CHI + h, 8, stride=4), :] for h in range(4)]
        for j in range(4):
            moved = [pltpu.roll(rows[h], CHI * ((h - j) % 4), 1) if h != j else rows[h] for h in range(4)]
            low = jnp.where(group == 0, moved[0], moved[1])
            high = jnp.where(group == 2, moved[2], moved[3])
            a = 16 * (c // 4) + 4 * j + c % 4
            second[a * 8 : a * 8 + 8, :] = jnp.where(group < 2, low, high)
    return [second[pl.ds(c, CHI, stride=8), :] for c in range(CHUNKS)]


def split_rows(chunks):
    pairs = [halves(c) for c in chunks]
    high = jnp.concatenate([p[0] for p in pairs], axis=1)
    low = jnp.concatenate([p[1] for p in pairs], axis=1)
    return jnp.concatenate([high, low], axis=0).astype(BF)


def split_lanes(chunks):
    high, low = halves(jnp.concatenate(chunks, axis=0))
    return jnp.concatenate([high, low], axis=1).astype(BF)


def left_multiply(matrix, split):
    high, low = halves(matrix)
    left = jnp.where(lane_group(matrix.shape) < 2, high, low).astype(BF)
    right = jnp.concatenate([split, split], axis=0)
    out = jnp.dot(left, right, preferred_element_type=F32)
    return [out[:, LANES * c : LANES * (c + 1)] for c in range(CHUNKS)]


def right_multiply(split, matrix):
    shape = (LANES, LANES)
    keep = lax.broadcasted_iota(jnp.int32, shape, 0) // CHI == lane_group(shape)
    blocks = [
        jnp.where(keep, jnp.concatenate([part] * 4, axis=0), 0.0).astype(BF) for part in halves(matrix)
    ]
    row = jnp.concatenate(blocks, axis=1)
    out = jnp.dot(split, jnp.concatenate([row, row], axis=0), preferred_element_type=F32)
    out = out[:, :LANES] + out[:, LANES:]
    return [out[CHI * c : CHI * (c + 1)] for c in range(CHUNKS)]


def contract(left, right):
    high, low = right[:CHI], right[CHI:]
    wide = jnp.concatenate([high, high, low, low], axis=0)
    out = lax.dot_general(left, wide, (((1,), (1,)), ((), ())), preferred_element_type=F32)
    out = out[:CHI] + out[CHI:]
    return out + pltpu.roll(out, LANES // 2, 1)


def normalize(matrix):
    row = lax.broadcasted_iota(jnp.int32, matrix.shape, 0)
    lane = lax.broadcasted_iota(jnp.int32, matrix.shape, 1)
    diagonal = jnp.where(row == lane, matrix, 0.0)
    trace = jnp.sum(jnp.sum(diagonal, axis=0, keepdims=True), axis=1, keepdims=True)
    return matrix * (CHI / trace)


def grow_all(natural_splits, moved_splits, envs, pairs):
    turned = [left_multiply(env[0], moved) for env, moved in zip(envs, moved_splits)]
    turned = [swap(chunks, *pair) for chunks, pair in zip(turned, pairs)]
    both = [right_multiply(split_lanes(chunks), env[1]) for chunks, env in zip(turned, envs)]
    raw = [contract(split_rows(chunks), natural) for chunks, natural in zip(both, natural_splits)]
    return [normalize(matrix) for matrix in raw]


def load_chunks(ref):
    return [ref[:, LANES * c : LANES * (c + 1)] for c in range(CHUNKS)]


def scratch_pairs(count):
    return [pltpu.VMEM((CHUNKS * CHI, LANES), F32)] * (2 * count)


def in_pairs(refs):
    return [tuple(refs[2 * i : 2 * i + 2]) for i in range(len(refs) // 2)]


def full_spec():
    return pl.BlockSpec(memory_space=pltpu.VMEM)


def scalar_spec():
    return pl.BlockSpec(memory_space=pltpu.SMEM)


def shape_of(*shape, dtype=F32):
    return jax.ShapeDtypeStruct(shape, dtype)


ENV = (CHI, LANES)
MESSAGE = (72, LANES)
GRAM = slice(CHI, CHI + 8)
ROWS = (2 * CHI, CHI2)
WIDE = (CHUNKS * CHI, 2 * LANES)
HALF = (CHI, CHI2 // 2)


def kernel_call(kernel, outs, scalars, args, scratch, nanos):
    return pl.pallas_call(
        kernel,
        out_shape=outs,
        in_specs=[scalar_spec()] * len(scalars) + [full_spec()] * len(args),
        out_specs=[full_spec()] * len(outs),
        scratch_shapes=scratch,
        cost_estimate=pl.CostEstimate(flops=int(nanos * 1150000), bytes_accessed=1024, transcendentals=0),
        compiler_params=pltpu.CompilerParams(vmem_limit_bytes=24 * 1024 * 1024),
    )(*scalars, *args)


def bond_rows(bond_ref, mask):
    return pl.ds(pl.multiple_of(8 * (bond_ref[0] ^ mask), 8), 8)


def assemble_kernel(bond_ref, *refs):
    *pieces, now_ref, later_ref = refs
    for mask, piece in zip(BOND_MASKS, pieces):
        rows = bond_rows(bond_ref, mask)
        now_ref[rows, :] = piece[LEAVES_DEV - 1, :, : CHI2 // 2]
        later_ref[rows, :] = piece[LEAVES_DEV - 1, :, CHI2 // 2 :]


def interleave(low, high, width):
    chunks = []
    lane = lax.broadcasted_iota(jnp.int32, (CHI, LANES), 1)
    for c in range(CHUNKS):
        if width >= LANES:
            block, rest = LANES * c // width, LANES * c % width
            part = high if block % 2 else low
            chunks.append(part[(block // 2 * width + rest) // LANES])
            continue
        base = LANES // 2 * (c % 2)
        out = None
        for block in range(LANES // width):
            part = (high if block % 2 else low)[c // 2]
            shift = (block * width - base - block // 2 * width) % LANES
            moved = pltpu.roll(part, shift, 1) if shift else part
            out = moved if out is None else jnp.where(lane < block * width, out, moved)
        chunks.append(out)
    return chunks


def every_other(chunks, width, parity):
    half = len(chunks) // 2
    if width >= LANES:
        step = width // LANES
        return [c for i, c in enumerate(chunks) if i // step % 2 == parity]
    lane = lax.broadcasted_iota(jnp.int32, (CHI, LANES), 1)
    groups = LANES // width
    result = []
    for i in range(half):
        out = None
        for j in range(groups):
            source = 2 * j + parity
            shift = (j - source) * width % LANES
            part = chunks[2 * i + source // groups]
            moved = pltpu.roll(part, shift, 1) if shift else part
            out = moved if out is None else jnp.where(lane < j * width, out, moved)
        result.append(out)
    return result


def merge_kernel(width, upper_ref, mine_ref, theirs_ref, after_ref, now_ref, *later_refs):
    upper = upper_ref[0] == 1
    mine = [mine_ref[:, LANES * c : LANES * (c + 1)] for c in range(CHUNKS // 2)]
    theirs = [theirs_ref[:, LANES * c : LANES * (c + 1)] for c in range(CHUNKS // 2)]
    low = [jnp.where(upper, t, m) for m, t in zip(mine, theirs)]
    high = [jnp.where(upper, m, t) for m, t in zip(mine, theirs)]
    for parity, out_ref in enumerate((now_ref, *later_refs)):
        out = every_other(low, width, parity) + every_other(high, width, parity)
        for c, chunk in enumerate(out):
            out_ref[:, LANES * c : LANES * (c + 1)] = chunk


def merge(width, upper, mine, theirs, after, last):
    outs = [shape_of(*HALF)] * (1 if last else 2)
    return kernel_call(
        functools.partial(merge_kernel, width), outs, (upper,), (mine, theirs, after), [], 300
    )


def prepare_kernel(width, core_ref, upper_ref, mine_ref, *refs):
    *their_refs, natural_ref, moved_ref, own_ref, other_ref = refs[:-6]
    pairs = in_pairs(refs[-6:])
    core = core_ref[0] == 1
    half = CHUNKS // 2
    mine = [mine_ref[:, LANES * c : LANES * (c + 1)] for c in range(half)]
    theirs = [
        jnp.concatenate([ref[:, LANES * c : LANES * (c + 1)] for ref in their_refs], axis=0) for c in range(half)
    ]
    low = [jnp.where(core, t, m) for m, t in zip(mine, theirs)]
    high = [jnp.where(core, m, t) for m, t in zip(mine, theirs)]
    natural = interleave(low, high, width)
    natural_ref[...] = split_rows(natural)
    by_left = swap_back(transposed(natural), *pairs[0])
    moved_ref[...] = split_rows(swap(natural, *pairs[1]))
    by_right = swap(by_left, *pairs[2])
    upper = upper_ref[0] == 1
    own = [jnp.where(upper, r, l) for l, r in zip(by_left, by_right)]
    other = [jnp.where(upper, l, r) for l, r in zip(by_left, by_right)]
    own_ref[...] = split_lanes(own)
    other_ref[...] = split_rows(other)


def prepare(width, core, upper, mine, theirs):
    outs = [shape_of(*ROWS, dtype=BF), shape_of(*ROWS, dtype=BF), shape_of(*WIDE, dtype=BF), shape_of(*ROWS, dtype=BF)]
    return kernel_call(
        functools.partial(prepare_kernel, width), outs, (core, upper), (mine, *theirs), scratch_pairs(3), 1
    )


def grow_and_partner(upper, natural, moved, other, mine_ref, theirs_ref, pairs):
    mine, theirs = mine_ref[:CHI, :], theirs_ref[:CHI, :]
    left_env = jnp.where(upper, theirs, mine)
    right_env = jnp.where(upper, mine, theirs)
    turned = left_multiply(left_env, moved)
    partner = left_multiply(theirs, other)
    turned = swap(turned, *pairs[0])
    partner = swap(partner, *pairs[1])
    both = right_multiply(split_lanes(turned), right_env)
    return normalize(contract(split_rows(both), natural)), split_rows(partner)


def grow_kernel(upper_ref, natural_ref, moved_ref, other_ref, mine_ref, theirs_ref, *refs):
    (out_ref, partner_ref), scratch = refs[-6:-4], refs[-4:]
    env, partner = grow_and_partner(
        upper_ref[0] == 1, natural_ref[...], moved_ref[...], other_ref[...], mine_ref, theirs_ref, in_pairs(scratch)
    )
    out_ref[:CHI, :] = env
    out_ref[GRAM, :] = mine_ref[GRAM, :] + theirs_ref[GRAM, :]
    out_ref[GRAM.stop :, :] = jnp.zeros((MESSAGE[0] - GRAM.stop, LANES), F32)
    partner_ref[...] = partner


def grow_level(upper, natural, moved, other, mine, theirs, *after):
    return kernel_call(
        grow_kernel,
        [shape_of(*MESSAGE), shape_of(*ROWS, dtype=BF)],
        (upper,),
        (natural, moved, other, mine, theirs, *after),
        scratch_pairs(2),
        900,
    )


def local_kernel(root_width, bond_ref, leaf_ref, *refs):
    *pieces, iso_ref, env_ref, message_ref = refs[:-6]
    pairs = in_pairs(refs[-6:])
    first = pairs[0][0]
    nodes = LEAVES_DEV - 1
    for mask, piece in zip(BOND_MASKS, pieces):
        rows = bond_rows(bond_ref, mask)
        for node in range(nodes):
            iso_ref[node, rows, :] = piece[node]
        first[rows, :] = piece[nodes, :, CHI2 - LANES :]
    lane = lax.broadcasted_iota(jnp.int32, (CHI, LANES), 1)
    root = split_rows([jnp.where(lane >= LANES - root_width, first[:CHI, :], 0.0)])
    gram = contract(root, root)
    naturals = [load_chunks(iso_ref.at[node]) for node in range(nodes)]
    moved = [split_rows(swap(natural, *pair)) for natural, pair in zip(naturals, pairs)]
    splits = [split_rows(natural) for natural in naturals]
    envs = grow_all(splits[:2], moved[:2], [(leaf_ref[2 * node], leaf_ref[2 * node + 1]) for node in range(2)], pairs)
    env_ref[0] = envs[0]
    env_ref[1] = envs[1]
    message_ref[:CHI, :] = grow_all(splits[2:], moved[2:], [envs], pairs)[0]
    message_ref[GRAM, :] = flat(gram, first)
    message_ref[GRAM.stop :, :] = jnp.zeros((MESSAGE[0] - GRAM.stop, LANES), F32)


def local_edges_kernel(node, leaf_ref, env_ref, iso_ref, after_ref, own_ref, partner_ref, *scratch):
    pairs = in_pairs(scratch)
    by_left = swap_back(transposed(load_chunks(iso_ref.at[node])), *pairs[0])
    if node < 2:
        left_env, right_env = leaf_ref[2 * node], leaf_ref[2 * node + 1]
    else:
        left_env, right_env = env_ref[0], env_ref[1]
    for_right = left_multiply(left_env, split_rows(by_left))
    by_right = swap(by_left, *pairs[1])
    partner_ref[1] = split_rows(swap(for_right, *pairs[2]))
    for_left = left_multiply(right_env, split_rows(by_right))
    own_ref[0] = split_lanes(by_left)
    own_ref[1] = split_lanes(by_right)
    partner_ref[0] = split_rows(swap(for_left, *pairs[3]))


def local_edges(node, *args):
    return kernel_call(
        functools.partial(local_edges_kernel, node),
        [shape_of(2, *WIDE, dtype=BF), shape_of(2, *ROWS, dtype=BF)],
        (),
        args,
        scratch_pairs(4),
        800,
    )


def flat(matrix, first):
    first[0:CHI, :] = matrix
    group = lane_group((8, LANES))
    rows = [first[pl.ds(h, 8, stride=4), :] for h in range(4)]
    return jnp.where(group < 2, jnp.where(group == 0, rows[0], rows[1]), jnp.where(group == 2, rows[2], rows[3]))


def unflat(flattened, first):
    group = lane_group((8, LANES))
    for h in range(4):
        part = jnp.where(group == h, flattened, 0.0)
        part = part + pltpu.roll(part, CHI, 1)
        first[pl.ds(h, 8, stride=4), :] = part + pltpu.roll(part, 2 * CHI, 1)
    return first[0:CHI, :]


def write_flat(out_ref, index, flattened):
    for c in range(CHUNKS):
        out_ref[index, 0:1, LANES * c : LANES * (c + 1)] = flattened[c : c + 1, :]


def descend(edges):
    mixed = [split_rows(right_multiply(own, state)) for own, _, state in edges]
    raw = [contract(left, partner) for left, (_, partner, _) in zip(mixed, edges)]
    return [normalize(matrix) for matrix in raw]


def down_kernel(levels, marked_ref, upper_ref, natural_ref, moved_ref, other_ref, mine_ref, theirs_ref, *refs):
    own_refs, partner_refs, refs = refs[:levels], refs[levels : 2 * levels - 1], refs[2 * levels - 1 :]
    local_own, local_partner, (leaf_out, inner_out, top_out) = refs[:3], refs[3:6], refs[6:9]
    first, *rooms = refs[9:-4]
    root_env, partner = grow_and_partner(
        upper_ref[0] == 1, natural_ref[...], moved_ref[...], other_ref[...], mine_ref, theirs_ref, in_pairs(refs[-4:])
    )
    state = normalize(unflat(mine_ref[GRAM, :] + theirs_ref[GRAM, :], first))
    top = root_env
    for level in range(levels - 1, -1, -1):
        top = jnp.where(marked_ref[level] == 1, state, top)
        split = partner if level == levels - 1 else partner_refs[level][...]
        state = descend([(own_refs[level][...], split, state)])[0]
    inner = descend([(local_own[2][side], local_partner[2][side], state) for side in range(2)])
    leaves = descend(
        [(local_own[leaf // 2][leaf % 2], local_partner[leaf // 2][leaf % 2], inner[leaf // 2]) for leaf in range(LEAVES_DEV)]
    )
    matrices = [top, *inner, state, *leaves]
    rows = [flat(matrix, room) for matrix, room in zip(matrices, rooms)]
    write_flat(top_out, 0, rows[0])
    for node in range(3):
        write_flat(inner_out, node, rows[1 + node])
    for leaf in range(LEAVES_DEV):
        for c in range(CHUNKS):
            leaf_out[leaf : leaf + 1, LANES * c : LANES * (c + 1)] = rows[4 + leaf][c : c + 1, :]


def exchange(value, mask):
    pairs = [(source, source ^ mask) for source in range(lax.axis_size("leaf"))]
    return lax.ppermute(value, "leaf", pairs)


def core_exchange(value):
    return [exchange(part, 1) for part in (value[: CHI // 2], value[CHI // 2 :])]


def bond_pieces(value):
    size = lax.axis_size("bond")
    return [value] + [
        lax.ppermute(value, "bond", [(source, source ^ mask) for source in range(size)])
        for mask in BOND_MASKS[1:]
    ]


def body(leaf_metric, local_iso, top_iso):
    devices = lax.axis_size("leaf")
    top_levels = devices.bit_length() - 1
    masks = [1, 2, 4, 12, 16, 48]
    position = lax.axis_index("leaf")
    bits = [(position >> level & 1).astype(jnp.int32).reshape(1) for level in range(top_levels)]
    bond = lax.axis_index("bond").astype(jnp.int32).reshape(1)
    leaves = jnp.tile(leaf_metric.reshape(LEAVES_DEV, CHI, CHI), (1, 1, 4))

    pieces = bond_pieces(jnp.concatenate([local_iso, top_iso], axis=0))
    now, later = kernel_call(assemble_kernel, [shape_of(*HALF)] * 2, (bond,), pieces, [], 200)
    other_half = core_exchange(now)
    local_whole, local_envs, message = kernel_call(
        functools.partial(local_kernel, CHI2 // devices),
        [shape_of(LEAVES_DEV - 1, CHI, CHI2), shape_of(2, *ENV), shape_of(*MESSAGE)],
        (bond,),
        (leaves, *pieces),
        scratch_pairs(3),
        1800,
    )

    owns, partners = [], []
    for level in range(top_levels):
        if level + 1 < top_levels:
            incoming = exchange(later, masks[level + 1])
        if level:
            other_half = core_exchange(now)
        natural, moved, own, other = prepare(CHI2 >> level + 1, bits[0], bits[level], now, other_half)
        theirs = exchange(message, masks[level])
        if level == top_levels - 1:
            owns.append(own)
            break
        if level == 0:
            early = merge(CHI2 >> 2, bits[1], later, incoming, message, False)
            before = early[:1]
        elif level == 3:
            local_edges_2 = local_edges(2, leaves, local_envs, local_whole, message)
            before = local_edges_2[:1]
        else:
            before = ()
        message, partner = grow_level(bits[level], natural, moved, other, message, theirs, *before)
        if level + 1 < top_levels:
            last = level + 2 == top_levels
            if level == 0:
                now, *rest = early
            else:
                now, *rest = merge(CHI2 >> level + 2, bits[level + 1], later, incoming, message, last)
            later = None if last else rest[0]
        owns.append(own)
        partners.append(partner)
    edges = [local_edges(node, leaves, local_envs, local_whole, message) for node in range(2)]
    local_own, local_partner = zip(*edges, local_edges_2)

    marked = jnp.stack(
        [((position + 1) % (2 << level) == 1 << level).astype(jnp.int32) for level in range(top_levels)]
    )
    leaf_rho, inner_rho, top_rho = kernel_call(
        functools.partial(down_kernel, top_levels),
        [shape_of(LEAVES_DEV, CHI2), shape_of(LEAVES_DEV - 1, 1, CHI2), shape_of(1, 1, CHI2)],
        (marked, bits[-1]),
        (natural, moved, other, message, theirs, *owns, *partners, *local_own, *local_partner),
        [pltpu.VMEM((CHI, LANES), F32)] * 9 + scratch_pairs(2),
        7000,
    )
    return (leaf_rho[None], jnp.swapaxes(inner_rho, 0, 1), top_rho)


def solution(mesh):
    in_specs = (P("bond", "leaf", None), P("leaf", "bond", None), P("leaf", "bond", None))
    out_specs = (P("bond", "leaf", None), P("bond", "leaf", None), P("bond", "leaf", None))
    return jax.shard_map(body, mesh=mesh, in_specs=in_specs, out_specs=out_specs, check_vma=False)
```

```python
import functools

import jax
import jax.numpy as jnp
from jax import lax
from jax.experimental import pallas as pl
from jax.experimental.pallas import tpu as pltpu
from jax.sharding import PartitionSpec as P

CHI = 32
LEAVES_DEV = 4
CHI2 = 1024
LANES = 128
CHUNKS = CHI2 // LANES
BOND_MASKS = (0, 2, 3, 1)
BF = jnp.bfloat16
F32 = jnp.float32


def lane_group(shape):
    return lax.broadcasted_iota(jnp.int32, shape, len(shape) - 1) // CHI


def halves(x):
    high = x.astype(BF).astype(F32)
    return high, x - high


def swap(chunks, first, second):
    for c in range(CHUNKS):
        first[c * CHI : (c + 1) * CHI, :] = chunks[c]
    group = lane_group((8, LANES))
    for c in range(CHUNKS):
        rows = [first[pl.ds(c * CHI + h, 8, stride=4), :] for h in range(4)]
        for g in range(4):
            moved = [pltpu.roll(rows[h], CHI * ((h - g) % 4), 1) if h != g else rows[h] for h in range(4)]
            low = jnp.where(group == 0, moved[0], moved[1])
            high = jnp.where(group == 2, moved[2], moved[3])
            second[(4 * c + g) * 8 : (4 * c + g) * 8 + 8, :] = jnp.where(group < 2, low, high)
    return [second[pl.ds(c, CHI, stride=8), :] for c in range(CHUNKS)]


def transposed(chunks):
    result = []
    for i in range(2):
        block = jnp.concatenate(chunks[4 * i : 4 * i + 4], axis=0).T
        result += [block[CHI * g : CHI * (g + 1)] for g in range(4)]
    return result


def swap_back(chunks, first, second):
    for c in range(CHUNKS):
        first[c * CHI : (c + 1) * CHI, :] = chunks[c]
    group = lane_group((8, LANES))
    for c in range(CHUNKS):
        rows = [first[pl.ds(c * CHI + h, 8, stride=4), :] for h in range(4)]
        for j in range(4):
            moved = [pltpu.roll(rows[h], CHI * ((h - j) % 4), 1) if h != j else rows[h] for h in range(4)]
            low = jnp.where(group == 0, moved[0], moved[1])
            high = jnp.where(group == 2, moved[2], moved[3])
            a = 16 * (c // 4) + 4 * j + c % 4
            second[a * 8 : a * 8 + 8, :] = jnp.where(group < 2, low, high)
    return [second[pl.ds(c, CHI, stride=8), :] for c in range(CHUNKS)]


def split_rows(chunks):
    pairs = [halves(c) for c in chunks]
    high = jnp.concatenate([p[0] for p in pairs], axis=1)
    low = jnp.concatenate([p[1] for p in pairs], axis=1)
    return jnp.concatenate([high, low], axis=0).astype(BF)


def split_lanes(chunks):
    high, low = halves(jnp.concatenate(chunks, axis=0))
    return jnp.concatenate([high, low], axis=1).astype(BF)


def left_multiply(matrix, split):
    high, low = halves(matrix)
    left = jnp.where(lane_group(matrix.shape) < 2, high, low).astype(BF)
    right = jnp.concatenate([split, split], axis=0)
    out = jnp.dot(left, right, preferred_element_type=F32)
    return [out[:, LANES * c : LANES * (c + 1)] for c in range(CHUNKS)]


def right_multiply(split, matrix):
    shape = (LANES, LANES)
    keep = lax.broadcasted_iota(jnp.int32, shape, 0) // CHI == lane_group(shape)
    blocks = [
        jnp.where(keep, jnp.concatenate([part] * 4, axis=0), 0.0).astype(BF) for part in halves(matrix)
    ]
    row = jnp.concatenate(blocks, axis=1)
    out = jnp.dot(split, jnp.concatenate([row, row], axis=0), preferred_element_type=F32)
    out = out[:, :LANES] + out[:, LANES:]
    return [out[CHI * c : CHI * (c + 1)] for c in range(CHUNKS)]


def contract(left, right):
    high, low = right[:CHI], right[CHI:]
    wide = jnp.concatenate([high, high, low, low], axis=0)
    out = lax.dot_general(left, wide, (((1,), (1,)), ((), ())), preferred_element_type=F32)
    out = out[:CHI] + out[CHI:]
    return out + pltpu.roll(out, LANES // 2, 1)


def normalize(matrix):
    row = lax.broadcasted_iota(jnp.int32, matrix.shape, 0)
    lane = lax.broadcasted_iota(jnp.int32, matrix.shape, 1)
    diagonal = jnp.where(row == lane, matrix, 0.0)
    trace = jnp.sum(jnp.sum(diagonal, axis=0, keepdims=True), axis=1, keepdims=True)
    return matrix * (CHI / trace)


def grow_all(natural_splits, moved_splits, envs, pairs):
    turned = [left_multiply(env[0], moved) for env, moved in zip(envs, moved_splits)]
    turned = [swap(chunks, *pair) for chunks, pair in zip(turned, pairs)]
    both = [right_multiply(split_lanes(chunks), env[1]) for chunks, env in zip(turned, envs)]
    raw = [contract(split_rows(chunks), natural) for chunks, natural in zip(both, natural_splits)]
    return [normalize(matrix) for matrix in raw]


def load_chunks(ref):
    return [ref[:, LANES * c : LANES * (c + 1)] for c in range(CHUNKS)]


def scratch_pairs(count):
    return [pltpu.VMEM((CHUNKS * CHI, LANES), F32)] * (2 * count)


def in_pairs(refs):
    return [tuple(refs[2 * i : 2 * i + 2]) for i in range(len(refs) // 2)]


def full_spec():
    return pl.BlockSpec(memory_space=pltpu.VMEM)


def scalar_spec():
    return pl.BlockSpec(memory_space=pltpu.SMEM)


def shape_of(*shape, dtype=F32):
    return jax.ShapeDtypeStruct(shape, dtype)


ENV = (CHI, LANES)
MESSAGE = (72, LANES)
GRAM = slice(CHI, CHI + 8)
ROWS = (2 * CHI, CHI2)
WIDE = (CHUNKS * CHI, 2 * LANES)
HALF = (CHI, CHI2 // 2)


def kernel_call(kernel, outs, scalars, args, scratch, nanos):
    return pl.pallas_call(
        kernel,
        out_shape=outs,
        in_specs=[scalar_spec()] * len(scalars) + [full_spec()] * len(args),
        out_specs=[full_spec()] * len(outs),
        scratch_shapes=scratch,
        cost_estimate=pl.CostEstimate(flops=int(nanos * 1150000), bytes_accessed=1024, transcendentals=0),
        compiler_params=pltpu.CompilerParams(vmem_limit_bytes=24 * 1024 * 1024),
    )(*scalars, *args)


def bond_rows(bond_ref, mask):
    return pl.ds(pl.multiple_of(8 * (bond_ref[0] ^ mask), 8), 8)


def assemble_kernel(bond_ref, *refs):
    *pieces, now_ref, later_ref = refs
    for mask, piece in zip(BOND_MASKS, pieces):
        rows = bond_rows(bond_ref, mask)
        now_ref[rows, :] = piece[LEAVES_DEV - 1, :, : CHI2 // 2]
        later_ref[rows, :] = piece[LEAVES_DEV - 1, :, CHI2 // 2 :]


def interleave(low, high, width):
    chunks = []
    lane = lax.broadcasted_iota(jnp.int32, (CHI, LANES), 1)
    for c in range(CHUNKS):
        if width >= LANES:
            block, rest = LANES * c // width, LANES * c % width
            part = high if block % 2 else low
            chunks.append(part[(block // 2 * width + rest) // LANES])
            continue
        base = LANES // 2 * (c % 2)
        out = None
        for block in range(LANES // width):
            part = (high if block % 2 else low)[c // 2]
            shift = (block * width - base - block // 2 * width) % LANES
            moved = pltpu.roll(part, shift, 1) if shift else part
            out = moved if out is None else jnp.where(lane < block * width, out, moved)
        chunks.append(out)
    return chunks


def every_other(chunks, width, parity):
    half = len(chunks) // 2
    if width >= LANES:
        step = width // LANES
        return [c for i, c in enumerate(chunks) if i // step % 2 == parity]
    lane = lax.broadcasted_iota(jnp.int32, (CHI, LANES), 1)
    groups = LANES // width
    result = []
    for i in range(half):
        out = None
        for j in range(groups):
            source = 2 * j + parity
            shift = (j - source) * width % LANES
            part = chunks[2 * i + source // groups]
            moved = pltpu.roll(part, shift, 1) if shift else part
            out = moved if out is None else jnp.where(lane < j * width, out, moved)
        result.append(out)
    return result


def merge_kernel(width, upper_ref, mine_ref, theirs_ref, after_ref, now_ref, *later_refs):
    upper = upper_ref[0] == 1
    mine = [mine_ref[:, LANES * c : LANES * (c + 1)] for c in range(CHUNKS // 2)]
    theirs = [theirs_ref[:, LANES * c : LANES * (c + 1)] for c in range(CHUNKS // 2)]
    low = [jnp.where(upper, t, m) for m, t in zip(mine, theirs)]
    high = [jnp.where(upper, m, t) for m, t in zip(mine, theirs)]
    for parity, out_ref in enumerate((now_ref, *later_refs)):
        out = every_other(low, width, parity) + every_other(high, width, parity)
        for c, chunk in enumerate(out):
            out_ref[:, LANES * c : LANES * (c + 1)] = chunk


def merge(width, upper, mine, theirs, after, last):
    outs = [shape_of(*HALF)] * (1 if last else 2)
    return kernel_call(
        functools.partial(merge_kernel, width), outs, (upper,), (mine, theirs, after), [], 300
    )


def prepare_kernel(width, core_ref, upper_ref, mine_ref, *refs):
    *their_refs, natural_ref, moved_ref, own_ref, other_ref = refs[:-6]
    pairs = in_pairs(refs[-6:])
    core = core_ref[0] == 1
    half = CHUNKS // 2
    mine = [mine_ref[:, LANES * c : LANES * (c + 1)] for c in range(half)]
    theirs = [
        jnp.concatenate([ref[:, LANES * c : LANES * (c + 1)] for ref in their_refs], axis=0) for c in range(half)
    ]
    low = [jnp.where(core, t, m) for m, t in zip(mine, theirs)]
    high = [jnp.where(core, m, t) for m, t in zip(mine, theirs)]
    natural = interleave(low, high, width)
    natural_ref[...] = split_rows(natural)
    by_left = swap_back(transposed(natural), *pairs[0])
    moved_ref[...] = split_rows(swap(natural, *pairs[1]))
    by_right = swap(by_left, *pairs[2])
    upper = upper_ref[0] == 1
    own = [jnp.where(upper, r, l) for l, r in zip(by_left, by_right)]
    other = [jnp.where(upper, l, r) for l, r in zip(by_left, by_right)]
    own_ref[...] = split_lanes(own)
    other_ref[...] = split_rows(other)


def prepare(width, core, upper, mine, theirs):
    outs = [shape_of(*ROWS, dtype=BF), shape_of(*ROWS, dtype=BF), shape_of(*WIDE, dtype=BF), shape_of(*ROWS, dtype=BF)]
    return kernel_call(
        functools.partial(prepare_kernel, width), outs, (core, upper), (mine, *theirs), scratch_pairs(3), 1
    )


def grow_and_partner(upper, natural, moved, other, mine_ref, theirs_ref, pairs):
    mine, theirs = mine_ref[:CHI, :], theirs_ref[:CHI, :]
    left_env = jnp.where(upper, theirs, mine)
    right_env = jnp.where(upper, mine, theirs)
    turned = left_multiply(left_env, moved)
    partner = left_multiply(theirs, other)
    turned = swap(turned, *pairs[0])
    partner = swap(partner, *pairs[1])
    both = right_multiply(split_lanes(turned), right_env)
    return normalize(contract(split_rows(both), natural)), split_rows(partner)


def grow_kernel(upper_ref, natural_ref, moved_ref, other_ref, mine_ref, theirs_ref, *refs):
    (out_ref, partner_ref), scratch = refs[-6:-4], refs[-4:]
    env, partner = grow_and_partner(
        upper_ref[0] == 1, natural_ref[...], moved_ref[...], other_ref[...], mine_ref, theirs_ref, in_pairs(scratch)
    )
    out_ref[:CHI, :] = env
    out_ref[GRAM, :] = mine_ref[GRAM, :] + theirs_ref[GRAM, :]
    out_ref[GRAM.stop :, :] = jnp.zeros((MESSAGE[0] - GRAM.stop, LANES), F32)
    partner_ref[...] = partner


def grow_level(upper, natural, moved, other, mine, theirs, *after):
    return kernel_call(
        grow_kernel,
        [shape_of(*MESSAGE), shape_of(*ROWS, dtype=BF)],
        (upper,),
        (natural, moved, other, mine, theirs, *after),
        scratch_pairs(2),
        900,
    )


def local_kernel(root_width, bond_ref, leaf_ref, *refs):
    *pieces, iso_ref, env_ref, message_ref = refs[:-6]
    pairs = in_pairs(refs[-6:])
    first = pairs[0][0]
    nodes = LEAVES_DEV - 1
    for mask, piece in zip(BOND_MASKS, pieces):
        rows = bond_rows(bond_ref, mask)
        for node in range(nodes):
            iso_ref[node, rows, :] = piece[node]
        first[rows, :] = piece[nodes, :, CHI2 - LANES :]
    lane = lax.broadcasted_iota(jnp.int32, (CHI, LANES), 1)
    root = split_rows([jnp.where(lane >= LANES - root_width, first[:CHI, :], 0.0)])
    gram = contract(root, root)
    naturals = [load_chunks(iso_ref.at[node]) for node in range(nodes)]
    moved = [split_rows(swap(natural, *pair)) for natural, pair in zip(naturals, pairs)]
    splits = [split_rows(natural) for natural in naturals]
    envs = grow_all(splits[:2], moved[:2], [(leaf_ref[2 * node], leaf_ref[2 * node + 1]) for node in range(2)], pairs)
    env_ref[0] = envs[0]
    env_ref[1] = envs[1]
    message_ref[:CHI, :] = grow_all(splits[2:], moved[2:], [envs], pairs)[0]
    message_ref[GRAM, :] = flat(gram, first)
    message_ref[GRAM.stop :, :] = jnp.zeros((MESSAGE[0] - GRAM.stop, LANES), F32)


def local_edges_kernel(node, leaf_ref, env_ref, iso_ref, after_ref, own_ref, partner_ref, *scratch):
    pairs = in_pairs(scratch)
    by_left = swap_back(transposed(load_chunks(iso_ref.at[node])), *pairs[0])
    if node < 2:
        left_env, right_env = leaf_ref[2 * node], leaf_ref[2 * node + 1]
    else:
        left_env, right_env = env_ref[0], env_ref[1]
    for_right = left_multiply(left_env, split_rows(by_left))
    by_right = swap(by_left, *pairs[1])
    partner_ref[1] = split_rows(swap(for_right, *pairs[2]))
    for_left = left_multiply(right_env, split_rows(by_right))
    own_ref[0] = split_lanes(by_left)
    own_ref[1] = split_lanes(by_right)
    partner_ref[0] = split_rows(swap(for_left, *pairs[3]))


def local_edges(node, *args):
    return kernel_call(
        functools.partial(local_edges_kernel, node),
        [shape_of(2, *WIDE, dtype=BF), shape_of(2, *ROWS, dtype=BF)],
        (),
        args,
        scratch_pairs(4),
        800,
    )


def flat(matrix, first):
    first[0:CHI, :] = matrix
    group = lane_group((8, LANES))
    rows = [first[pl.ds(h, 8, stride=4), :] for h in range(4)]
    return jnp.where(group < 2, jnp.where(group == 0, rows[0], rows[1]), jnp.where(group == 2, rows[2], rows[3]))


def unflat(flattened, first):
    group = lane_group((8, LANES))
    for h in range(4):
        part = jnp.where(group == h, flattened, 0.0)
        part = part + pltpu.roll(part, CHI, 1)
        first[pl.ds(h, 8, stride=4), :] = part + pltpu.roll(part, 2 * CHI, 1)
    return first[0:CHI, :]


def write_flat(out_ref, index, flattened):
    for c in range(CHUNKS):
        out_ref[index, 0:1, LANES * c : LANES * (c + 1)] = flattened[c : c + 1, :]


def descend(edges):
    mixed = [split_rows(right_multiply(own, state)) for own, _, state in edges]
    raw = [contract(left, partner) for left, (_, partner, _) in zip(mixed, edges)]
    return [normalize(matrix) for matrix in raw]


def down_kernel(levels, marked_ref, upper_ref, natural_ref, moved_ref, other_ref, mine_ref, theirs_ref, *refs):
    own_refs, partner_refs, refs = refs[:levels], refs[levels : 2 * levels - 1], refs[2 * levels - 1 :]
    local_own, local_partner, (leaf_out, inner_out, top_out) = refs[:3], refs[3:6], refs[6:9]
    first, *rooms = refs[9:-4]
    pairs = in_pairs(refs[-4:])
    upper = upper_ref[0] == 1
    mine, theirs = mine_ref[:CHI, :], theirs_ref[:CHI, :]
    partner = split_rows(swap(left_multiply(theirs, other_ref[...]), *pairs[1]))
    state = normalize(unflat(mine_ref[GRAM, :] + theirs_ref[GRAM, :], first))
    steps = [
        lambda _: left_multiply(jnp.where(upper, theirs, mine), moved_ref[...]),
        lambda turned: swap(turned, *pairs[0]),
        lambda turned: right_multiply(split_lanes(turned), jnp.where(upper, mine, theirs)),
        lambda both: normalize(contract(split_rows(both), natural_ref[...])),
    ]
    root_env = None
    states = []
    for level in range(levels - 1, -1, -1):
        states.append(state)
        if steps:
            root_env = steps.pop(0)(root_env)
        split = partner if level == levels - 1 else partner_refs[level][...]
        state = descend([(own_refs[level][...], split, state)])[0]
    top = root_env
    for level in range(levels):
        top = jnp.where(marked_ref[level] == 1, states[levels - 1 - level], top)
    inner = descend([(local_own[2][side], local_partner[2][side], state) for side in range(2)])
    leaves = descend(
        [(local_own[leaf // 2][leaf % 2], local_partner[leaf // 2][leaf % 2], inner[leaf // 2]) for leaf in range(LEAVES_DEV)]
    )
    matrices = [top, *inner, state, *leaves]
    rows = [flat(matrix, room) for matrix, room in zip(matrices, rooms)]
    write_flat(top_out, 0, rows[0])
    for node in range(3):
        write_flat(inner_out, node, rows[1 + node])
    for leaf in range(LEAVES_DEV):
        for c in range(CHUNKS):
            leaf_out[leaf : leaf + 1, LANES * c : LANES * (c + 1)] = rows[4 + leaf][c : c + 1, :]


def exchange(value, mask):
    pairs = [(source, source ^ mask) for source in range(lax.axis_size("leaf"))]
    return lax.ppermute(value, "leaf", pairs)


def core_exchange(value):
    return [exchange(part, 1) for part in (value[: CHI // 2], value[CHI // 2 :])]


def bond_pieces(value):
    size = lax.axis_size("bond")
    return [value] + [
        lax.ppermute(value, "bond", [(source, source ^ mask) for source in range(size)])
        for mask in BOND_MASKS[1:]
    ]


def body(leaf_metric, local_iso, top_iso):
    devices = lax.axis_size("leaf")
    top_levels = devices.bit_length() - 1
    masks = [1, 2, 4, 12, 16, 48]
    position = lax.axis_index("leaf")
    bits = [(position >> level & 1).astype(jnp.int32).reshape(1) for level in range(top_levels)]
    bond = lax.axis_index("bond").astype(jnp.int32).reshape(1)
    leaves = jnp.tile(leaf_metric.reshape(LEAVES_DEV, CHI, CHI), (1, 1, 4))

    pieces = bond_pieces(jnp.concatenate([local_iso, top_iso], axis=0))
    now, later = kernel_call(assemble_kernel, [shape_of(*HALF)] * 2, (bond,), pieces, [], 200)
    other_half = core_exchange(now)
    local_whole, local_envs, message = kernel_call(
        functools.partial(local_kernel, CHI2 // devices),
        [shape_of(LEAVES_DEV - 1, CHI, CHI2), shape_of(2, *ENV), shape_of(*MESSAGE)],
        (bond,),
        (leaves, *pieces),
        scratch_pairs(3),
        1800,
    )

    owns, partners = [], []
    for level in range(top_levels):
        if level + 1 < top_levels:
            incoming = exchange(later, masks[level + 1])
        if level:
            other_half = core_exchange(now)
        natural, moved, own, other = prepare(CHI2 >> level + 1, bits[0], bits[level], now, other_half)
        theirs = exchange(message, masks[level])
        if level == top_levels - 1:
            owns.append(own)
            break
        if level == 0:
            early = merge(CHI2 >> 2, bits[1], later, incoming, message, False)
            before = early[:1]
        elif level == 3:
            local_edges_2 = local_edges(2, leaves, local_envs, local_whole, message)
            before = local_edges_2[:1]
        else:
            before = ()
        message, partner = grow_level(bits[level], natural, moved, other, message, theirs, *before)
        if level + 1 < top_levels:
            last = level + 2 == top_levels
            if level == 0:
                now, *rest = early
            else:
                now, *rest = merge(CHI2 >> level + 2, bits[level + 1], later, incoming, message, last)
            later = None if last else rest[0]
        owns.append(own)
        partners.append(partner)
    edges = [local_edges(node, leaves, local_envs, local_whole, message) for node in range(2)]
    local_own, local_partner = zip(*edges, local_edges_2)

    marked = jnp.stack(
        [((position + 1) % (2 << level) == 1 << level).astype(jnp.int32) for level in range(top_levels)]
    )
    leaf_rho, inner_rho, top_rho = kernel_call(
        functools.partial(down_kernel, top_levels),
        [shape_of(LEAVES_DEV, CHI2), shape_of(LEAVES_DEV - 1, 1, CHI2), shape_of(1, 1, CHI2)],
        (marked, bits[-1]),
        (natural, moved, other, message, theirs, *owns, *partners, *local_own, *local_partner),
        [pltpu.VMEM((CHI, LANES), F32)] * 9 + scratch_pairs(2),
        7000,
    )
    return (leaf_rho[None], jnp.swapaxes(inner_rho, 0, 1), top_rho)


def solution(mesh):
    in_specs = (P("bond", "leaf", None), P("leaf", "bond", None), P("leaf", "bond", None))
    out_specs = (P("bond", "leaf", None), P("bond", "leaf", None), P("bond", "leaf", None))
    return jax.shard_map(body, mesh=mesh, in_specs=in_specs, out_specs=out_specs, check_vma=False)
```

```python
import functools

import jax
import jax.numpy as jnp
from jax import lax
from jax.experimental import pallas as pl
from jax.experimental.pallas import tpu as pltpu
from jax.sharding import PartitionSpec as P

CHI = 32
LEAVES_DEV = 4
CHI2 = 1024
LANES = 128
CHUNKS = CHI2 // LANES
BOND_MASKS = (0, 2, 3, 1)
BF = jnp.bfloat16
F32 = jnp.float32


def lane_group(shape):
    return lax.broadcasted_iota(jnp.int32, shape, len(shape) - 1) // CHI


def halves(x):
    high = x.astype(BF).astype(F32)
    return high, x - high


def swap(chunks, first, second):
    for c in range(CHUNKS):
        first[c * CHI : (c + 1) * CHI, :] = chunks[c]
    group = lane_group((8, LANES))
    for c in range(CHUNKS):
        rows = [first[pl.ds(c * CHI + h, 8, stride=4), :] for h in range(4)]
        for g in range(4):
            moved = [pltpu.roll(rows[h], CHI * ((h - g) % 4), 1) if h != g else rows[h] for h in range(4)]
            low = jnp.where(group == 0, moved[0], moved[1])
            high = jnp.where(group == 2, moved[2], moved[3])
            second[(4 * c + g) * 8 : (4 * c + g) * 8 + 8, :] = jnp.where(group < 2, low, high)
    return [second[pl.ds(c, CHI, stride=8), :] for c in range(CHUNKS)]


def transposed(chunks):
    result = []
    for i in range(2):
        block = jnp.concatenate(chunks[4 * i : 4 * i + 4], axis=0).T
        result += [block[CHI * g : CHI * (g + 1)] for g in range(4)]
    return result


def swap_back(chunks, first, second):
    for c in range(CHUNKS):
        first[c * CHI : (c + 1) * CHI, :] = chunks[c]
    group = lane_group((8, LANES))
    for c in range(CHUNKS):
        rows = [first[pl.ds(c * CHI + h, 8, stride=4), :] for h in range(4)]
        for j in range(4):
            moved = [pltpu.roll(rows[h], CHI * ((h - j) % 4), 1) if h != j else rows[h] for h in range(4)]
            low = jnp.where(group == 0, moved[0], moved[1])
            high = jnp.where(group == 2, moved[2], moved[3])
            a = 16 * (c // 4) + 4 * j + c % 4
            second[a * 8 : a * 8 + 8, :] = jnp.where(group < 2, low, high)
    return [second[pl.ds(c, CHI, stride=8), :] for c in range(CHUNKS)]


def split_rows(chunks):
    pairs = [halves(c) for c in chunks]
    high = jnp.concatenate([p[0] for p in pairs], axis=1)
    low = jnp.concatenate([p[1] for p in pairs], axis=1)
    return jnp.concatenate([high, low], axis=0).astype(BF)


def split_lanes(chunks):
    high, low = halves(jnp.concatenate(chunks, axis=0))
    return jnp.concatenate([high, low], axis=1).astype(BF)


def left_multiply(matrix, split):
    high, low = halves(matrix)
    left = jnp.where(lane_group(matrix.shape) < 2, high, low).astype(BF)
    right = jnp.concatenate([split, split], axis=0)
    out = jnp.dot(left, right, preferred_element_type=F32)
    return [out[:, LANES * c : LANES * (c + 1)] for c in range(CHUNKS)]


def right_multiply(split, matrix):
    shape = (LANES, LANES)
    keep = lax.broadcasted_iota(jnp.int32, shape, 0) // CHI == lane_group(shape)
    blocks = [
        jnp.where(keep, jnp.concatenate([part] * 4, axis=0), 0.0).astype(BF) for part in halves(matrix)
    ]
    row = jnp.concatenate(blocks, axis=1)
    out = jnp.dot(split, jnp.concatenate([row, row], axis=0), preferred_element_type=F32)
    out = out[:, :LANES] + out[:, LANES:]
    return [out[CHI * c : CHI * (c + 1)] for c in range(CHUNKS)]


def contract(left, right):
    high, low = right[:CHI], right[CHI:]
    wide = jnp.concatenate([high, high, low, low], axis=0)
    out = lax.dot_general(left, wide, (((1,), (1,)), ((), ())), preferred_element_type=F32)
    out = out[:CHI] + out[CHI:]
    return out + pltpu.roll(out, LANES // 2, 1)


def normalize(matrix):
    row = lax.broadcasted_iota(jnp.int32, matrix.shape, 0)
    lane = lax.broadcasted_iota(jnp.int32, matrix.shape, 1)
    diagonal = jnp.where(row == lane, matrix, 0.0)
    trace = jnp.sum(jnp.sum(diagonal, axis=0, keepdims=True), axis=1, keepdims=True)
    return matrix * (CHI / trace)


def grow_all(natural_splits, moved_splits, envs, pairs):
    turned = [left_multiply(env[0], moved) for env, moved in zip(envs, moved_splits)]
    turned = [swap(chunks, *pair) for chunks, pair in zip(turned, pairs)]
    both = [right_multiply(split_lanes(chunks), env[1]) for chunks, env in zip(turned, envs)]
    raw = [contract(split_rows(chunks), natural) for chunks, natural in zip(both, natural_splits)]
    return [normalize(matrix) for matrix in raw]


def load_chunks(ref):
    return [ref[:, LANES * c : LANES * (c + 1)] for c in range(CHUNKS)]


def scratch_pairs(count):
    return [pltpu.VMEM((CHUNKS * CHI, LANES), F32)] * (2 * count)


def in_pairs(refs):
    return [tuple(refs[2 * i : 2 * i + 2]) for i in range(len(refs) // 2)]


def full_spec():
    return pl.BlockSpec(memory_space=pltpu.VMEM)


def scalar_spec():
    return pl.BlockSpec(memory_space=pltpu.SMEM)


def shape_of(*shape, dtype=F32):
    return jax.ShapeDtypeStruct(shape, dtype)


ENV = (CHI, LANES)
MESSAGE = (72, LANES)
GRAM = slice(CHI, CHI + 8)
ROWS = (2 * CHI, CHI2)
WIDE = (CHUNKS * CHI, 2 * LANES)
HALF = (CHI, CHI2 // 2)


def kernel_call(kernel, outs, scalars, args, scratch, nanos):
    return pl.pallas_call(
        kernel,
        out_shape=outs,
        in_specs=[scalar_spec()] * len(scalars) + [full_spec()] * len(args),
        out_specs=[full_spec()] * len(outs),
        scratch_shapes=scratch,
        cost_estimate=pl.CostEstimate(flops=int(nanos * 1150000), bytes_accessed=1024, transcendentals=0),
        compiler_params=pltpu.CompilerParams(vmem_limit_bytes=24 * 1024 * 1024),
    )(*scalars, *args)


def bond_rows(bond_ref, mask):
    return pl.ds(pl.multiple_of(8 * (bond_ref[0] ^ mask), 8), 8)


def assemble_kernel(bond_ref, *refs):
    *pieces, now_ref, later_ref = refs
    for mask, piece in zip(BOND_MASKS, pieces):
        rows = bond_rows(bond_ref, mask)
        now_ref[rows, :] = piece[LEAVES_DEV - 1, :, : CHI2 // 2]
        later_ref[rows, :] = piece[LEAVES_DEV - 1, :, CHI2 // 2 :]


def interleave(low, high, width):
    chunks = []
    lane = lax.broadcasted_iota(jnp.int32, (CHI, LANES), 1)
    for c in range(CHUNKS):
        if width >= LANES:
            block, rest = LANES * c // width, LANES * c % width
            part = high if block % 2 else low
            chunks.append(part[(block // 2 * width + rest) // LANES])
            continue
        base = LANES // 2 * (c % 2)
        out = None
        for block in range(LANES // width):
            part = (high if block % 2 else low)[c // 2]
            shift = (block * width - base - block // 2 * width) % LANES
            moved = pltpu.roll(part, shift, 1) if shift else part
            out = moved if out is None else jnp.where(lane < block * width, out, moved)
        chunks.append(out)
    return chunks


def every_other(chunks, width, parity):
    half = len(chunks) // 2
    if width >= LANES:
        step = width // LANES
        return [c for i, c in enumerate(chunks) if i // step % 2 == parity]
    lane = lax.broadcasted_iota(jnp.int32, (CHI, LANES), 1)
    groups = LANES // width
    result = []
    for i in range(half):
        out = None
        for j in range(groups):
            source = 2 * j + parity
            shift = (j - source) * width % LANES
            part = chunks[2 * i + source // groups]
            moved = pltpu.roll(part, shift, 1) if shift else part
            out = moved if out is None else jnp.where(lane < j * width, out, moved)
        result.append(out)
    return result


def merge_kernel(width, upper_ref, mine_ref, theirs_ref, after_ref, now_ref, *later_refs):
    upper = upper_ref[0] == 1
    parts = mine_ref.shape[1] // LANES
    mine = [mine_ref[:, LANES * c : LANES * (c + 1)] for c in range(parts)]
    theirs = [theirs_ref[:, LANES * c : LANES * (c + 1)] for c in range(parts)]
    low = [jnp.where(upper, t, m) for m, t in zip(mine, theirs)]
    high = [jnp.where(upper, m, t) for m, t in zip(mine, theirs)]
    for parity, out_ref in enumerate((now_ref, *later_refs)):
        if later_refs:
            out = every_other(low, width, parity) + every_other(high, width, parity)
        else:
            out = low + high
        if out_ref.shape[1] == CHI2 // 4:
            out = every_other(out, width // 2, 0)
        for c, chunk in enumerate(out):
            out_ref[:, LANES * c : LANES * (c + 1)] = chunk


def merge(width, upper, mine, theirs, after, later_columns):
    outs = [shape_of(*HALF)] + [shape_of(CHI, later_columns)] * (later_columns > 0)
    return kernel_call(
        functools.partial(merge_kernel, width), outs, (upper,), (mine, theirs, after), [], 300
    )


def prepare_kernel(width, core_ref, upper_ref, mine_ref, *refs):
    *their_refs, natural_ref, moved_ref, own_ref, other_ref = refs[:-6]
    pairs = in_pairs(refs[-6:])
    core = core_ref[0] == 1
    half = CHUNKS // 2
    mine = [mine_ref[:, LANES * c : LANES * (c + 1)] for c in range(half)]
    theirs = [
        jnp.concatenate([ref[:, LANES * c : LANES * (c + 1)] for ref in their_refs], axis=0) for c in range(half)
    ]
    low = [jnp.where(core, t, m) for m, t in zip(mine, theirs)]
    high = [jnp.where(core, m, t) for m, t in zip(mine, theirs)]
    natural = interleave(low, high, width)
    natural_ref[...] = split_rows(natural)
    by_left = swap_back(transposed(natural), *pairs[0])
    moved_ref[...] = split_rows(swap(natural, *pairs[1]))
    by_right = swap(by_left, *pairs[2])
    upper = upper_ref[0] == 1
    own = [jnp.where(upper, r, l) for l, r in zip(by_left, by_right)]
    other = [jnp.where(upper, l, r) for l, r in zip(by_left, by_right)]
    own_ref[...] = split_lanes(own)
    other_ref[...] = split_rows(other)


def prepare(width, core, upper, mine, theirs):
    outs = [shape_of(*ROWS, dtype=BF), shape_of(*ROWS, dtype=BF), shape_of(*WIDE, dtype=BF), shape_of(*ROWS, dtype=BF)]
    return kernel_call(
        functools.partial(prepare_kernel, width), outs, (core, upper), (mine, *theirs), scratch_pairs(3), 1
    )


def grow_and_partner(upper, natural, moved, other, mine_ref, theirs_ref, pairs):
    mine, theirs = mine_ref[:CHI, :], theirs_ref[:CHI, :]
    left_env = jnp.where(upper, theirs, mine)
    right_env = jnp.where(upper, mine, theirs)
    turned = left_multiply(left_env, moved)
    partner = left_multiply(theirs, other)
    turned = swap(turned, *pairs[0])
    partner = swap(partner, *pairs[1])
    both = right_multiply(split_lanes(turned), right_env)
    return normalize(contract(split_rows(both), natural)), split_rows(partner)


def grow_kernel(upper_ref, natural_ref, moved_ref, other_ref, mine_ref, theirs_ref, *refs):
    (out_ref, partner_ref), scratch = refs[-6:-4], refs[-4:]
    env, partner = grow_and_partner(
        upper_ref[0] == 1, natural_ref[...], moved_ref[...], other_ref[...], mine_ref, theirs_ref, in_pairs(scratch)
    )
    out_ref[:CHI, :] = env
    out_ref[GRAM, :] = mine_ref[GRAM, :] + theirs_ref[GRAM, :]
    out_ref[GRAM.stop :, :] = jnp.zeros((MESSAGE[0] - GRAM.stop, LANES), F32)
    partner_ref[...] = partner


def grow_level(upper, natural, moved, other, mine, theirs, *after):
    return kernel_call(
        grow_kernel,
        [shape_of(*MESSAGE), shape_of(*ROWS, dtype=BF)],
        (upper,),
        (natural, moved, other, mine, theirs, *after),
        scratch_pairs(2),
        900,
    )


def local_kernel(root_width, bond_ref, leaf_ref, *refs):
    *pieces, iso_ref, env_ref, message_ref = refs[:-6]
    pairs = in_pairs(refs[-6:])
    first = pairs[0][0]
    nodes = LEAVES_DEV - 1
    for mask, piece in zip(BOND_MASKS, pieces):
        rows = bond_rows(bond_ref, mask)
        for node in range(nodes):
            iso_ref[node, rows, :] = piece[node]
        first[rows, :] = piece[nodes, :, CHI2 - LANES :]
    lane = lax.broadcasted_iota(jnp.int32, (CHI, LANES), 1)
    root = split_rows([jnp.where(lane >= LANES - root_width, first[:CHI, :], 0.0)])
    gram = contract(root, root)
    naturals = [load_chunks(iso_ref.at[node]) for node in range(nodes)]
    moved = [split_rows(swap(natural, *pair)) for natural, pair in zip(naturals, pairs)]
    splits = [split_rows(natural) for natural in naturals]
    envs = grow_all(splits[:2], moved[:2], [(leaf_ref[2 * node], leaf_ref[2 * node + 1]) for node in range(2)], pairs)
    env_ref[0] = envs[0]
    env_ref[1] = envs[1]
    message_ref[:CHI, :] = grow_all(splits[2:], moved[2:], [envs], pairs)[0]
    message_ref[GRAM, :] = flat(gram, first)
    message_ref[GRAM.stop :, :] = jnp.zeros((MESSAGE[0] - GRAM.stop, LANES), F32)


def local_edges_kernel(node, leaf_ref, env_ref, iso_ref, after_ref, own_ref, partner_ref, *scratch):
    pairs = in_pairs(scratch)
    by_left = swap_back(transposed(load_chunks(iso_ref.at[node])), *pairs[0])
    if node < 2:
        left_env, right_env = leaf_ref[2 * node], leaf_ref[2 * node + 1]
    else:
        left_env, right_env = env_ref[0], env_ref[1]
    for_right = left_multiply(left_env, split_rows(by_left))
    by_right = swap(by_left, *pairs[1])
    partner_ref[1] = split_rows(swap(for_right, *pairs[2]))
    for_left = left_multiply(right_env, split_rows(by_right))
    own_ref[0] = split_lanes(by_left)
    own_ref[1] = split_lanes(by_right)
    partner_ref[0] = split_rows(swap(for_left, *pairs[3]))


def local_edges(node, *args):
    return kernel_call(
        functools.partial(local_edges_kernel, node),
        [shape_of(2, *WIDE, dtype=BF), shape_of(2, *ROWS, dtype=BF)],
        (),
        args,
        scratch_pairs(4),
        800,
    )


def flat(matrix, first):
    first[0:CHI, :] = matrix
    group = lane_group((8, LANES))
    rows = [first[pl.ds(h, 8, stride=4), :] for h in range(4)]
    return jnp.where(group < 2, jnp.where(group == 0, rows[0], rows[1]), jnp.where(group == 2, rows[2], rows[3]))


def unflat(flattened, first):
    group = lane_group((8, LANES))
    for h in range(4):
        part = jnp.where(group == h, flattened, 0.0)
        part = part + pltpu.roll(part, CHI, 1)
        first[pl.ds(h, 8, stride=4), :] = part + pltpu.roll(part, 2 * CHI, 1)
    return first[0:CHI, :]


def write_flat(out_ref, index, flattened):
    for c in range(CHUNKS):
        out_ref[index, 0:1, LANES * c : LANES * (c + 1)] = flattened[c : c + 1, :]


def descend(edges):
    mixed = [split_rows(right_multiply(own, state)) for own, _, state in edges]
    raw = [contract(left, partner) for left, (_, partner, _) in zip(mixed, edges)]
    return [normalize(matrix) for matrix in raw]


def down_kernel(levels, marked_ref, upper_ref, natural_ref, moved_ref, other_ref, mine_ref, theirs_ref, *refs):
    own_refs, partner_refs, refs = refs[:levels], refs[levels : 2 * levels - 1], refs[2 * levels - 1 :]
    local_own, local_partner, (leaf_out, inner_out, top_out) = refs[:3], refs[3:6], refs[6:9]
    first, *rooms = refs[9:-4]
    pairs = in_pairs(refs[-4:])
    upper = upper_ref[0] == 1
    mine, theirs = mine_ref[:CHI, :], theirs_ref[:CHI, :]
    partner = split_rows(swap(left_multiply(theirs, other_ref[...]), *pairs[1]))
    state = normalize(unflat(mine_ref[GRAM, :] + theirs_ref[GRAM, :], first))
    steps = [
        lambda _: left_multiply(jnp.where(upper, theirs, mine), moved_ref[...]),
        lambda turned: swap(turned, *pairs[0]),
        lambda turned: right_multiply(split_lanes(turned), jnp.where(upper, mine, theirs)),
        lambda both: normalize(contract(split_rows(both), natural_ref[...])),
    ]
    root_env = None
    states = []
    for level in range(levels - 1, -1, -1):
        states.append(state)
        if steps:
            root_env = steps.pop(0)(root_env)
        split = partner if level == levels - 1 else partner_refs[level][...]
        state = descend([(own_refs[level][...], split, state)])[0]
    top = root_env
    for level in range(levels):
        top = jnp.where(marked_ref[level] == 1, states[levels - 1 - level], top)
    inner = descend([(local_own[2][side], local_partner[2][side], state) for side in range(2)])
    leaves = descend(
        [(local_own[leaf // 2][leaf % 2], local_partner[leaf // 2][leaf % 2], inner[leaf // 2]) for leaf in range(LEAVES_DEV)]
    )
    matrices = [top, *inner, state, *leaves]
    rows = [flat(matrix, room) for matrix, room in zip(matrices, rooms)]
    write_flat(top_out, 0, rows[0])
    for node in range(3):
        write_flat(inner_out, node, rows[1 + node])
    for leaf in range(LEAVES_DEV):
        for c in range(CHUNKS):
            leaf_out[leaf : leaf + 1, LANES * c : LANES * (c + 1)] = rows[4 + leaf][c : c + 1, :]


def exchange(value, mask):
    pairs = [(source, source ^ mask) for source in range(lax.axis_size("leaf"))]
    return lax.ppermute(value, "leaf", pairs)


def core_exchange(value):
    return [exchange(part, 1) for part in (value[: CHI // 2], value[CHI // 2 :])]


def bond_pieces(value):
    size = lax.axis_size("bond")
    return [value] + [
        lax.ppermute(value, "bond", [(source, source ^ mask) for source in range(size)])
        for mask in BOND_MASKS[1:]
    ]


def body(leaf_metric, local_iso, top_iso):
    devices = lax.axis_size("leaf")
    top_levels = devices.bit_length() - 1
    masks = [1, 2, 4, 12, 16, 48]
    position = lax.axis_index("leaf")
    bits = [(position >> level & 1).astype(jnp.int32).reshape(1) for level in range(top_levels)]
    bond = lax.axis_index("bond").astype(jnp.int32).reshape(1)
    leaves = jnp.tile(leaf_metric.reshape(LEAVES_DEV, CHI, CHI), (1, 1, 4))

    pieces = bond_pieces(jnp.concatenate([local_iso, top_iso], axis=0))
    now, later = kernel_call(assemble_kernel, [shape_of(*HALF)] * 2, (bond,), pieces, [], 200)
    other_half = core_exchange(now)
    local_whole, local_envs, message = kernel_call(
        functools.partial(local_kernel, CHI2 // devices),
        [shape_of(LEAVES_DEV - 1, CHI, CHI2), shape_of(2, *ENV), shape_of(*MESSAGE)],
        (bond,),
        (leaves, *pieces),
        scratch_pairs(3),
        1800,
    )

    owns, partners = [], []
    for level in range(top_levels):
        if level + 1 < top_levels:
            incoming = exchange(later, masks[level + 1])
        if level:
            other_half = core_exchange(now)
        natural, moved, own, other = prepare(CHI2 >> level + 1, bits[0], bits[level], now, other_half)
        theirs = exchange(message, masks[level])
        if level == top_levels - 1:
            owns.append(own)
            break
        if level == 0:
            early = merge(CHI2 >> 2, bits[1], later, incoming, message, CHI2 // 2)
            before = early[:1]
        elif level == 3:
            local_edges_2 = local_edges(2, leaves, local_envs, local_whole, message)
            before = local_edges_2[:1]
        else:
            before = ()
        message, partner = grow_level(bits[level], natural, moved, other, message, theirs, *before)
        if level + 1 < top_levels:
            last = level + 2 == top_levels
            if level == 0:
                now, *rest = early
            else:
                columns = 0 if last else CHI2 // 4 if level + 3 == top_levels else CHI2 // 2
                now, *rest = merge(CHI2 >> level + 2, bits[level + 1], later, incoming, message, columns)
            later = None if last else rest[0]
        owns.append(own)
        partners.append(partner)
    edges = [local_edges(node, leaves, local_envs, local_whole, message) for node in range(2)]
    local_own, local_partner = zip(*edges, local_edges_2)

    marked = jnp.stack(
        [((position + 1) % (2 << level) == 1 << level).astype(jnp.int32) for level in range(top_levels)]
    )
    leaf_rho, inner_rho, top_rho = kernel_call(
        functools.partial(down_kernel, top_levels),
        [shape_of(LEAVES_DEV, CHI2), shape_of(LEAVES_DEV - 1, 1, CHI2), shape_of(1, 1, CHI2)],
        (marked, bits[-1]),
        (natural, moved, other, message, theirs, *owns, *partners, *local_own, *local_partner),
        [pltpu.VMEM((CHI, LANES), F32)] * 9 + scratch_pairs(2),
        7000,
    )
    return (leaf_rho[None], jnp.swapaxes(inner_rho, 0, 1), top_rho)


def solution(mesh):
    in_specs = (P("bond", "leaf", None), P("leaf", "bond", None), P("leaf", "bond", None))
    out_specs = (P("bond", "leaf", None), P("bond", "leaf", None), P("bond", "leaf", None))
    return jax.shard_map(body, mesh=mesh, in_specs=in_specs, out_specs=out_specs, check_vma=False)
```
